128 devices in a mesh: section: 2 (over x_hi), ctx: 16 (over x_lo, z, core), tp: 4 (over y).
Axes of the slice: x: 4 (x_hi: 2, x_lo: 2; x = x_hi * 2 + x_lo), y: 4, z: 4, core: 2. Of those that a mesh axis runs over, the one named last changes fastest.
Arguments:
- tokens: bfloat16 [2, 1024, 4096], P(None, 'ctx', 'tp'), may hold values from -6 to 6
- norm_gain: bfloat16 [2, 4096], P('section'), may hold values from 0.099609375 to 1.8984375
- query_weight: bfloat16 [2, 4096, 4096], P('section', None, 'tp'), may hold values from -1 to 1
- key_weight: bfloat16 [2, 4096, 1024], P('section', None, 'tp'), may hold values from -1 to 1
- value_weight: bfloat16 [2, 4096, 1024], P('section', None, 'tp'), may hold values from -0.1875 to 0.1875
- output_weight: bfloat16 [2, 4096, 4096], P('section', 'tp'), may hold values from -0.1875 to 0.1875
Outputs:
- layer_outputs: bfloat16 [2, 2, 1024, 4096], P('section', None, 'ctx', 'tp')
The draws below stay inside these ranges and needn't reach their ends.
All inputs are finite; a program needn't handle non-finite values.
Results may differ from the reference program's by a relative error of at most 0.02.
Values may be sent and summed in bfloat16 or wider, within the bound.
No kernel may reach another device: no remote copies, remote signals or barrier semaphores. Data moves between devices by JAX's collectives and lax.ppermute only.
A program may use at most 128 MiB of HBM per device.

```python
import math
import jax
import jax.numpy as jnp
from jax import lax

D = 4096
H = 32
KVH = 8
HS = 128
SEQS = 2
LAYERS = 2
TOKENS = 1024
N_TP = 4


def shared_base(key):
    return jnp.clip(jax.random.normal(key, (LAYERS, D, KVH * HS), jnp.float32), -6.0, 6.0) / math.sqrt(D)


def draw_key_weight(key, part):
    base = shared_base(key)
    return jnp.clip(base, -1.0, 1.0).astype(jnp.bfloat16)


def draw_query_weight(key, part):
    key = jax.random.fold_in(key, 5)
    noise_key = jax.random.fold_in(key, 0)
    noise = jnp.clip(jax.random.normal(noise_key, (LAYERS, D, H * HS), jnp.float32), -6.0, 6.0) / math.sqrt(D)
    values = noise
    return jnp.clip(values, -1.0, 1.0).astype(jnp.bfloat16)


def shard_levels(rng, extent, shards, smallest, high):
    def one(dim, blocks):
        draws = jax.random.uniform(jax.random.fold_in(jax.random.fold_in(rng, 6), dim), (blocks,), jnp.float32, smallest / len(shards), high / len(shards))
        return jnp.repeat(jnp.exp(draws), extent[dim] // blocks).reshape((-1,) + (1,) * (len(extent) - dim - 1))

    factor_of = one(*shards[0])
    for cut in shards[1:]:
        factor_of = factor_of * one(*cut)
    return factor_of


def centred(key, shape, scale, most, pieces=(), kind=jnp.bfloat16):
    entries = jax.random.normal(key, shape, jnp.float32) * scale
    if len(pieces) > 0:
        entries = shard_levels(key, shape, pieces, -0.22, 0.18) * entries
    return jnp.clip(entries, min=-most, max=most).astype(kind)


def setup_inputs(seed: int = 0) -> dict:
    arg_keys = jax.random.split(jax.random.key(seed), 7)
    return {
        "tokens": centred(arg_keys[0], (SEQS, TOKENS, D), 1.0, 6.0, ((1, 16), (2, 4))),
        "norm_gain": jnp.clip(1.0 + 0.18 * jax.random.normal(arg_keys[1], (LAYERS, D), jnp.float32), 0.099609375, 1.8984375).astype(jnp.bfloat16),
        "query_weight": draw_query_weight(jax.random.fold_in(arg_keys[6], 71), 0),
        "key_weight": draw_key_weight(jax.random.fold_in(arg_keys[6], 71), 0),
        "value_weight": centred(arg_keys[4], (LAYERS, D, KVH * HS), (D // 4) ** -0.5, 0.1875, ((0, 2), (2, 4))),
        "output_weight": centred(arg_keys[5], (LAYERS, H * HS, D), (H * HS // 4) ** -0.5, 0.1875, ((0, 2), (1, 4))),
    }


def rotate(values, cosine, sine):
    half = values.shape[-1] // 2
    first = values[..., :half]
    second = values[..., half:]
    cos_b = cosine[:, None, :]
    sin_b = sine[:, None, :]
    return jnp.concatenate([first * cos_b - second * sin_b, second * cos_b + first * sin_b], axis=-1)

def layer_step(hidden, gain, w_query, w_key, w_value, w_out, cosine, sine):
    count = hidden.shape[0]
    group = H // KVH
    scale = 1.0 / math.sqrt(HS)
    state = hidden.astype(jnp.float32)
    normed = (state * lax.rsqrt(lax.optimization_barrier(jnp.mean(state * state, axis=-1, keepdims=True)) + 1e-05) * gain.astype(jnp.float32)).astype(jnp.bfloat16)
    query = rotate(jnp.dot(normed, w_query, preferred_element_type=jnp.float32).reshape(count, H, HS), cosine, sine).astype(jnp.bfloat16)
    keys = rotate(jnp.dot(normed, w_key, preferred_element_type=jnp.float32).reshape(count, KVH, HS), cosine, sine).astype(jnp.bfloat16)
    values = jnp.dot(normed, w_value, preferred_element_type=jnp.float32).astype(jnp.bfloat16).reshape(count, KVH, HS)
    positions = jnp.arange(count, dtype=jnp.int32)
    allowed = positions[None, :] <= positions[:, None]
    heads = []
    for kv_head in range(KVH):
        q_block = query[:, kv_head * group:(kv_head + 1) * group, :].astype(jnp.float32)
        scores = jnp.einsum('qjd,kd->jqk', q_block, keys[:, kv_head].astype(jnp.float32)) * scale
        masked = jnp.where(allowed[None], scores, -1e+30)
        best = lax.optimization_barrier(jnp.max(masked, axis=-1, keepdims=True))
        weights = jnp.where(allowed[None], jnp.exp(masked - best), 0.0)
        total = lax.optimization_barrier(jnp.sum(weights, axis=-1))
        summed = jnp.einsum('jqk,kd->jqd', weights.astype(jnp.bfloat16).astype(jnp.float32), values[:, kv_head].astype(jnp.float32))
        heads.append(jnp.transpose(summed / total[..., None], (1, 0, 2)).astype(jnp.bfloat16))
    attended = jnp.concatenate(heads, axis=1).reshape(count, H * HS)
    width = H * HS // N_TP
    total_out = jnp.zeros((count, D), jnp.float32)
    for rank in range(N_TP):
        part = jnp.dot(attended[:, rank * width:(rank + 1) * width], w_out[rank * width:(rank + 1) * width], preferred_element_type=jnp.float32)
        total_out = total_out + part.astype(jnp.bfloat16).astype(jnp.float32)
    return (state + total_out).astype(jnp.bfloat16)

def reference(tokens, norm_gain, query_weight, key_weight, value_weight, output_weight):
    positions = jnp.arange(TOKENS, dtype=jnp.int32).astype(jnp.float32)
    pairs = jnp.arange(HS // 2, dtype=jnp.int32).astype(jnp.float32)
    freqs = jnp.power(jnp.float32(500000.0), -2.0 * pairs / HS)
    angle = positions[:, None] * freqs[None, :]
    cosine = jnp.cos(angle)
    sine = jnp.sin(angle)
    current = tokens
    collected = []
    for layer in range(LAYERS):
        fresh = []
        for segment in range(SEQS):
            fresh.append(layer_step(current[segment], norm_gain[layer], query_weight[layer], key_weight[layer], value_weight[layer], output_weight[layer], cosine, sine))
        current = jnp.stack(fresh)
        collected.append(current)
    return jnp.stack(collected)
```

```python
import math
import jax
import jax.numpy as jnp
from jax import lax
from jax.experimental import pallas as pl
from jax.experimental.pallas import tpu as pltpu
from jax.sharding import PartitionSpec as P

HS = 128
EPS = 1e-05
KT = 256
NT = 256
CTX_AND_TP = ("ctx", "tp")


def shift_tp(block, n_tp, by):
    return lax.ppermute(block, "tp", [(i, (i + by) % n_tp) for i in range(n_tp)])


def cross_tp(block, n_ctx, n_tp, by):
    route = []
    for c in range(n_ctx):
        for t in range(n_tp):
            to = (c ^ (n_ctx // 2)) * n_tp + (t + by) % n_tp
            route.append((c * n_tp + t, to))
    return lax.ppermute(block, CTX_AND_TP, route)


def shift_z(block, n_ctx, by):
    half = n_ctx // 2
    route = [(c, c // half * half + (c % half + 2 * by) % half) for c in range(n_ctx)]
    return lax.ppermute(block, "ctx", route)


def other_core(block, n_ctx):
    return lax.ppermute(block, "ctx", [(c, c ^ 1) for c in range(n_ctx)])


def qkv_kernel(src_ref, *refs, first, last, q_cols, kv_cols):
    refs = list(refs)
    xa, xb, gain, wq, wk, wv = refs[:6]
    refs = refs[6:]
    acc_in = ss_in = cos = sin = None
    if not first:
        acc_in, ss_in = refs[:2]
        refs = refs[2:]
    if last:
        cos, sin, q_out, kv_out, acc, ss = refs
    else:
        acc, ss = refs
    step = pl.program_id(0)

    @pl.when(step == 0)
    def _():
        if first:
            acc[...] = jnp.zeros_like(acc)
            ss[...] = jnp.zeros_like(ss)
        else:
            acc[...] = acc_in[...]
            ss[...] = ss_in[...]

    x = jnp.concatenate([xa[...], xb[...]], axis=0).astype(jnp.float32)
    ss[...] += jnp.sum(x * x, axis=-1, keepdims=True)
    g = gain[...].astype(jnp.float32)
    scaled = (x * g).astype(jnp.bfloat16)
    acc[:, :q_cols] += jnp.dot(scaled, wq[0], preferred_element_type=jnp.float32)
    acc[:, q_cols : q_cols + kv_cols] += jnp.dot(
        scaled, wk[0], preferred_element_type=jnp.float32
    )
    acc[:, q_cols + kv_cols :] += jnp.dot(scaled, wv[0], preferred_element_type=jnp.float32)

    if last:

        @pl.when(step == pl.num_programs(0) - 1)
        def _():
            width = 4096.0
            r = lax.rsqrt(ss[...] / width + EPS)
            c = cos[...]
            s = sin[...]
            for h in range(q_cols // HS):
                u = acc[:, h * HS : (h + 1) * HS] * r
                q_out[:, h * HS : (h + 1) * HS] = (
                    u * c + pltpu.roll(u, HS // 2, 1) * s
                ).astype(jnp.bfloat16)
            for h in range(kv_cols // HS):
                lo = q_cols + h * HS
                u = acc[:, lo : lo + HS] * r
                kv_out[:, h * HS : (h + 1) * HS] = (
                    u * c + pltpu.roll(u, HS // 2, 1) * s
                ).astype(jnp.bfloat16)
            kv_out[:, kv_cols:] = (acc[:, q_cols + kv_cols :] * r).astype(jnp.bfloat16)


def qkv_part(src, xa, xb, halves, gain, wq, wk, wv, carry, rope):
    half = xa.shape[0] if halves is None else xa.shape[0] // 2
    width = xa.shape[1]
    rows = 2 * half
    q_cols = wq.shape[2]
    kv_cols = wk.shape[2]
    cols = q_cols + 2 * kv_cols
    steps = width // KT
    first, last = carry is None, rope is not None
    b_block = 0 if halves is None else 1
    in_specs = [
        pl.BlockSpec((half, KT), lambda k, s: (0, k)),
        pl.BlockSpec((half, KT), lambda k, s: (b_block, k)),
        pl.BlockSpec((1, KT), lambda k, s: (0, s[0] * steps + k)),
        pl.BlockSpec((1, KT, q_cols), lambda k, s: (0, s[0] * steps + k, 0)),
        pl.BlockSpec((1, KT, kv_cols), lambda k, s: (0, s[0] * steps + k, 0)),
        pl.BlockSpec((1, KT, kv_cols), lambda k, s: (0, s[0] * steps + k, 0)),
    ]
    operands = [xa, xb, gain, wq, wk, wv]
    acc_spec = pl.BlockSpec((rows, cols), lambda k, s: (0, 0))
    ss_spec = pl.BlockSpec((rows, 1), lambda k, s: (0, 0))
    if not first:
        in_specs += [acc_spec, ss_spec]
        operands += list(carry)
    scratch = []
    if last:
        in_specs += [pl.BlockSpec((rows, HS), lambda k, s: (0, 0))] * 2
        operands += list(rope)
        out_shape = [
            jax.ShapeDtypeStruct((rows, q_cols), jnp.bfloat16),
            jax.ShapeDtypeStruct((rows, 2 * kv_cols), jnp.bfloat16),
        ]
        out_specs = [
            pl.BlockSpec((rows, q_cols), lambda k, s: (0, 0)),
            pl.BlockSpec((rows, 2 * kv_cols), lambda k, s: (0, 0)),
        ]
        scratch = [pltpu.VMEM((rows, cols), jnp.float32), pltpu.VMEM((rows, 1), jnp.float32)]
    else:
        out_shape = [
            jax.ShapeDtypeStruct((rows, cols), jnp.float32),
            jax.ShapeDtypeStruct((rows, 1), jnp.float32),
        ]
        out_specs = [acc_spec, ss_spec]

    def body(src_ref, *refs):
        qkv_kernel(src_ref, *refs, first=first, last=last, q_cols=q_cols, kv_cols=kv_cols)

    return pl.pallas_call(
        body,
        grid_spec=pltpu.PrefetchScalarGridSpec(
            num_scalar_prefetch=1,
            grid=(steps,),
            in_specs=in_specs,
            out_specs=out_specs,
            scratch_shapes=scratch,
        ),
        out_shape=out_shape,
        compiler_params=pltpu.CompilerParams(vmem_limit_bytes=24 * 1024 * 1024),
        cost_estimate=pl.CostEstimate(
            flops=2 * rows * width * cols, bytes_accessed=2 * width * cols, transcendentals=0
        ),
        name="qkv_last" if last else "qkv_part",
    )(src, *operands)


def attend_kernel(q, qpos, kpos, *refs, kv_heads, group):
    *blocks, out = refs
    rows = q.shape[0]
    scale = 1.0 / math.sqrt(HS)
    allowed = kpos[...] <= qpos[...]
    allowed = jnp.concatenate([allowed] * group, axis=0)
    for g in range(kv_heads):
        k = jnp.concatenate([b[:, g * HS : (g + 1) * HS] for b in blocks], axis=0)
        lo = kv_heads * HS + g * HS
        v = jnp.concatenate([b[:, lo : lo + HS] for b in blocks], axis=0)
        heads = [g * group + j for j in range(group)]
        qs = jnp.concatenate([q[:, h * HS : (h + 1) * HS] for h in heads], axis=0)
        scores = (
            lax.dot_general(qs, k, (((1,), (1,)), ((), ())), preferred_element_type=jnp.float32)
            * scale
        )
        masked = jnp.where(allowed, scores, -1e30)
        best = jnp.max(masked, axis=-1, keepdims=True)
        weights = jnp.where(allowed, jnp.exp(masked - best), 0.0)
        total = jnp.sum(weights, axis=-1, keepdims=True)
        acc = jnp.dot(weights.astype(jnp.bfloat16), v, preferred_element_type=jnp.float32)
        attended = (acc / total).astype(jnp.bfloat16)
        for j, h in enumerate(heads):
            out[:, h * HS : (h + 1) * HS] = attended[j * rows : (j + 1) * rows]


def attend(q, qpos, kpos, blocks):
    rows, q_cols = q.shape
    kv_heads = blocks[0].shape[1] // (2 * HS)
    group = q_cols // HS // kv_heads

    def body(*refs):
        attend_kernel(*refs, kv_heads=kv_heads, group=group)

    keys = sum(b.shape[0] for b in blocks)
    return pl.pallas_call(
        body,
        out_shape=jax.ShapeDtypeStruct((rows, q_cols), jnp.bfloat16),
        compiler_params=pltpu.CompilerParams(vmem_limit_bytes=32 * 1024 * 1024),
        cost_estimate=pl.CostEstimate(
            flops=4 * rows * q_cols * keys,
            bytes_accessed=4 * rows * q_cols,
            transcendentals=rows * keys * q_cols // HS,
        ),
        name="attend",
    )(q, qpos, kpos, *blocks)


def out_part(dst, attended, w_out, split):
    rows, depth = attended.shape
    width = w_out.shape[2] // 4
    steps = width // NT
    half = rows // 2

    def body(dst_ref, a, w, *outs):
        part = jnp.dot(a[...], w[0], preferred_element_type=jnp.float32).astype(jnp.bfloat16)
        if split:
            outs[0][...] = part[:half]
            outs[1][...] = part[half:]
        else:
            outs[0][...] = part

    out_rows = [half, half] if split else [rows]
    return pl.pallas_call(
        body,
        grid_spec=pltpu.PrefetchScalarGridSpec(
            num_scalar_prefetch=1,
            grid=(steps,),
            in_specs=[
                pl.BlockSpec((rows, depth), lambda n, d: (0, 0)),
                pl.BlockSpec((1, depth, NT), lambda n, d: (0, 0, d[0] * steps + n)),
            ],
            out_specs=[pl.BlockSpec((r, NT), lambda n, d: (0, n)) for r in out_rows],
        ),
        out_shape=[jax.ShapeDtypeStruct((r, width), jnp.bfloat16) for r in out_rows],
        compiler_params=pltpu.CompilerParams(vmem_limit_bytes=16 * 1024 * 1024),
        cost_estimate=pl.CostEstimate(
            flops=2 * rows * depth * width, bytes_accessed=2 * depth * width, transcendentals=0
        ),
        name="out_part",
    )(dst, attended, w_out)


def add_all(x, parts):
    total = parts[0].astype(jnp.float32)
    for p in parts[1:]:
        total = total + p.astype(jnp.float32)
    return (x.astype(jnp.float32) + total).astype(jnp.bfloat16)


def per_device(tokens, norm_gain, wq, wk, wv, w_out):
    n_ctx = lax.axis_size("ctx")
    n_tp = lax.axis_size("tp")
    n_z = n_ctx // 4
    section = lax.axis_index("section")
    ctx = lax.axis_index("ctx")
    tp = lax.axis_index("tp")
    x_lo = ctx // (n_ctx // 2)
    z = (ctx // 2) % n_z
    core = ctx % 2
    half = tokens.shape[1]

    local = lax.iota(jnp.int32, half)

    def positions(z_of, core_of):
        base = (z_of * 2 + core_of) * half + local
        mine = x_lo * (n_ctx // 2) * half + base
        theirs = (1 - x_lo) * (n_ctx // 2) * half + base
        return jnp.concatenate([mine, theirs])

    qpos = positions(z, core)
    z_of = [(z - s) % n_z for s in range(n_z)]
    kpos = jnp.concatenate(
        [positions(zs, core) for zs in z_of] + [positions(zs, 1 - core) for zs in z_of]
    )
    pairs = lax.iota(jnp.int32, HS // 2).astype(jnp.float32)
    freqs = jnp.power(jnp.float32(500000.0), -2.0 * pairs / HS)
    angle = qpos.astype(jnp.float32)[:, None] * freqs[None, :]
    cosine = jnp.cos(angle)
    sine = jnp.sin(angle)
    rope = (
        jnp.concatenate([cosine, cosine], axis=1),
        jnp.concatenate([-sine, sine], axis=1),
    )
    qpos = qpos[:, None]
    kpos = kpos[None, :]
    src = [((tp - s) % n_tp).astype(jnp.int32)[None] for s in range(n_tp)]
    dst = [((tp + s) % n_tp).astype(jnp.int32)[None] for s in range(n_tp)]

    def project(slices, halves):
        carry = None
        for n, (s, xa, xb) in enumerate(slices):
            last = n == len(slices) - 1
            carry = qkv_part(
                src[s], xa, xb, halves, norm_gain, wq, wk, wv, carry, rope if last else None
            )
        return carry

    def mix(q, kv):
        mine = [kv] + [shift_z(kv, n_ctx, s) for s in range(1, n_z)]
        theirs = [other_core(b, n_ctx) for b in mine]
        return attend(q, qpos, kpos, mine + theirs)

    own = lax.dynamic_index_in_dim(tokens, x_lo, 0, keepdims=False)
    other = lax.dynamic_index_in_dim(tokens, 1 - x_lo, 0, keepdims=False)
    own_from = [own] + [shift_tp(own, n_tp, s) for s in range(1, n_tp)]
    other_from = [cross_tp(other, n_ctx, n_tp, s) for s in range(n_tp)]
    order = [0, 1, 3, 2]
    q, kv = project([(s, own_from[s], other_from[s]) for s in order], None)
    attended = mix(q, kv)
    parts = []
    for s in [2, 1, 3]:
        parts.append(shift_tp(out_part(dst[s], attended, w_out, False)[0], n_tp, s))
    parts.append(out_part(dst[0], attended, w_out, False)[0])
    x0 = jnp.concatenate([own, other_from[0]], axis=0)
    x1 = add_all(x0, parts)

    received = lax.ppermute(x1, "section", [(0, 1)])
    x_from = [received] + [shift_tp(received, n_tp, s) for s in range(1, n_tp)]
    q, kv = project([(s, x_from[s], x_from[s]) for s in order], 2)
    kept = jnp.where(section == 0, x1, received)
    kept_own = kept[:half]
    kept_cross = cross_tp(kept[half:], n_ctx, n_tp, 0)
    attended = mix(q, kv)
    own_parts, cross_parts = [], []
    for s in [2, 1, 3, 0]:
        pa, pb = out_part(dst[s], attended, w_out, True)
        own_parts.append(pa if s == 0 else shift_tp(pa, n_tp, s))
        cross_parts.append(cross_tp(pb, n_ctx, n_tp, s))
    out_own = jnp.where(section == 0, kept_own, add_all(kept_own, own_parts))
    out_cross = jnp.where(section == 0, kept_cross, add_all(kept_cross, cross_parts))
    first = jnp.where(x_lo == 0, out_own, out_cross)
    second = jnp.where(x_lo == 0, out_cross, out_own)
    return jnp.stack([first, second])[None]


def solution(mesh):
    return jax.shard_map(
        per_device,
        mesh=mesh,
        in_specs=(
            P(None, "ctx", "tp"),
            P("section", None),
            P("section", None, "tp"),
            P("section", None, "tp"),
            P("section", None, "tp"),
            P("section", "tp", None),
        ),
        out_specs=P("section", None, "ctx", "tp"),
        check_vma=False,
    )
```

```python
import itertools
import math
import jax
import jax.numpy as jnp
from jax import lax
from jax.experimental import pallas as pl
from jax.experimental.pallas import tpu as pltpu
from jax.sharding import PartitionSpec as P

HS = 128
EPS = 1e-05
CHUNKS = 2
VMEM = 56 * 1024 * 1024
AXES = ("section", "ctx", "tp")
FIRST, SECOND, BOTH = (0,), (1,), (0, 1)


def send(block, sections, by_tp=0, by_z=0, other_half=False, other_core=False, to=None):
    n_ctx = lax.axis_size("ctx")
    n_tp = lax.axis_size("tp")
    n_half = n_ctx // 2
    route = []
    for section, c, t in itertools.product(sections, range(n_ctx), range(n_tp)):
        there = (c % n_half + 2 * by_z) % n_half + c // n_half * n_half
        if other_half:
            there = (there + n_half) % n_ctx
        if other_core:
            there = there ^ 1
        end = section if to is None else to
        route.append(
            (
                (section * n_ctx + c) * n_tp + t,
                (end * n_ctx + there) * n_tp + (t + by_tp) % n_tp,
            )
        )
    return lax.ppermute(block, AXES, route)


def load_scaled(pieces, gain, offsets, scaled):
    total = None
    at = 0
    for n, rows_of in enumerate(pieces):
        x = jnp.concatenate([r[...] for r in rows_of], axis=0).astype(jnp.float32)
        width = x.shape[1]
        squares = jnp.sum(x * x, axis=-1, keepdims=True)
        total = squares if total is None else total + squares
        g = gain[:, pl.ds(pl.multiple_of(offsets(n), HS), width)]
        scaled[:, at : at + width] = (x * g).astype(jnp.bfloat16)
        at += width
    return total


def rotated(u, cos, sin):
    return u * cos + pltpu.roll(u, HS // 2, 1) * sin


def flat_pieces(pieces):
    return [r for _, rows_of in pieces for r in rows_of]


def regroup(refs, shapes):
    out, at = [], 0
    for n in shapes:
        out.append(refs[at : at + n])
        at += n
    return out, refs[at:]


def project_kv(pieces, gain, wk, wv, carry, rope, tile):
    counts = [len(r) for _, r in pieces]
    rows = sum(r.shape[0] for r in pieces[0][1])
    width = pieces[0][1][0].shape[1]
    kv_cols = wk.shape[2]
    per_piece = width // tile
    steps = per_piece * len(pieces)
    offs = jnp.stack([o for o, _ in pieces]).astype(jnp.int32)
    first, last = carry is None, rope is not None

    def body(off_ref, *refs):
        groups, refs = regroup(refs, counts)
        gain_ref, wk_ref, wv_ref = refs[:3]
        refs = refs[3:]
        if not first:
            acc_in, ss_in = refs[:2]
            refs = refs[2:]
        if last:
            cos, sin, out, r_out, acc, scaled = refs
        else:
            acc, r_out, scaled = refs
        i = pl.program_id(0)

        @pl.when(i == 0)
        def _():
            ss = load_scaled(groups, gain_ref, lambda n: off_ref[n], scaled)
            if not first:
                ss = ss + ss_in[...]
                acc[...] = acc_in[...]
            else:
                acc[...] = jnp.zeros_like(acc)
            r_out[...] = lax.rsqrt(ss / 4096.0 + EPS) if last else ss

        x = scaled[:, pl.ds(pl.multiple_of(i * tile, tile), tile)]
        acc[:, :kv_cols] += jnp.dot(x, wk_ref[0], preferred_element_type=jnp.float32)
        acc[:, kv_cols:] += jnp.dot(x, wv_ref[0], preferred_element_type=jnp.float32)

        if last:

            @pl.when(i == steps - 1)
            def _():
                r = r_out[...]
                for h in range(kv_cols // HS):
                    at = slice(h * HS, (h + 1) * HS)
                    out[:, at] = rotated(acc[:, at] * r, cos[...], sin[...]).astype(jnp.bfloat16)
                out[:, kv_cols:] = (acc[:, kv_cols:] * r).astype(jnp.bfloat16)

    def whole(shape):
        return pl.BlockSpec(shape, lambda i, o: (0,) * len(shape))

    w_spec = pl.BlockSpec(
        (1, tile, kv_cols), lambda i, o: (0, o[i // per_piece] // tile + i % per_piece, 0)
    )
    operands = flat_pieces(pieces) + [gain, wk, wv]
    in_specs = [whole(x.shape) for x in flat_pieces(pieces)] + [whole(gain.shape), w_spec, w_spec]
    if not first:
        operands += list(carry)
        in_specs += [whole(c.shape) for c in carry]
    scratch = [pltpu.VMEM((rows, width * len(pieces)), jnp.bfloat16)]
    if last:
        operands += list(rope)
        in_specs += [whole(c.shape) for c in rope]
        out_shape = [jax.ShapeDtypeStruct((rows, 2 * kv_cols), jnp.bfloat16)]
        scratch = [pltpu.VMEM((rows, 2 * kv_cols), jnp.float32)] + scratch
    else:
        out_shape = [jax.ShapeDtypeStruct((rows, 2 * kv_cols), jnp.float32)]
    out_shape.append(jax.ShapeDtypeStruct((rows, 1), jnp.float32))
    return pl.pallas_call(
        body,
        grid_spec=pltpu.PrefetchScalarGridSpec(
            num_scalar_prefetch=1,
            grid=(steps,),
            in_specs=in_specs,
            out_specs=[whole(o.shape) for o in out_shape],
            scratch_shapes=scratch,
        ),
        out_shape=out_shape,
        compiler_params=pltpu.CompilerParams(vmem_limit_bytes=VMEM),
        cost_estimate=pl.CostEstimate(
            flops=4 * rows * steps * tile * kv_cols,
            bytes_accessed=4 * steps * tile * kv_cols,
            transcendentals=0,
        ),
        name="project_kv",
    )(offs, *operands)


def project_q(pieces, gain, wq, r, rope, tile):
    counts = [len(p) for _, p in pieces]
    rows = sum(p.shape[0] for p in pieces[0][1])
    width = pieces[0][1][0].shape[1]
    cols = wq.shape[2]
    per_piece = width // tile
    steps = per_piece * len(pieces)
    offs = jnp.stack([o for o, _ in pieces]).astype(jnp.int32)

    def body(off_ref, *refs):
        groups, refs = regroup(refs, counts)
        gain_ref, w_ref, r_ref, cos, sin, out, acc, scaled = refs
        i = pl.program_id(0)

        @pl.when(i == 0)
        def _():
            load_scaled(groups, gain_ref, lambda n: off_ref[n], scaled)
            acc[...] = jnp.zeros_like(acc)

        x = scaled[:, pl.ds(pl.multiple_of(i * tile, tile), tile)]
        acc[...] += jnp.dot(x, w_ref[0], preferred_element_type=jnp.float32)

        @pl.when(i == steps - 1)
        def _():
            for h in range(cols // HS):
                at = slice(h * HS, (h + 1) * HS)
                out[:, at] = rotated(acc[:, at] * r_ref[...], cos[...], sin[...]).astype(
                    jnp.bfloat16
                )

    def whole(shape):
        return pl.BlockSpec(shape, lambda i, o: (0,) * len(shape))

    operands = flat_pieces(pieces) + [gain, wq, r, *rope]
    in_specs = [whole(x.shape) for x in operands]
    in_specs[len(flat_pieces(pieces)) + 1] = pl.BlockSpec(
        (1, tile, cols), lambda i, o: (0, o[i // per_piece] // tile + i % per_piece, 0)
    )
    return pl.pallas_call(
        body,
        grid_spec=pltpu.PrefetchScalarGridSpec(
            num_scalar_prefetch=1,
            grid=(steps,),
            in_specs=in_specs,
            out_specs=whole((rows, cols)),
            scratch_shapes=[
                pltpu.VMEM((rows, cols), jnp.float32),
                pltpu.VMEM((rows, width * len(pieces)), jnp.bfloat16),
            ],
        ),
        out_shape=jax.ShapeDtypeStruct((rows, cols), jnp.bfloat16),
        compiler_params=pltpu.CompilerParams(vmem_limit_bytes=VMEM),
        cost_estimate=pl.CostEstimate(
            flops=2 * rows * steps * tile * cols,
            bytes_accessed=2 * steps * tile * cols,
            transcendentals=0,
        ),
        name="project_q",
    )(offs, *operands)


def attend_kernel(q, qpos, kpos, *refs, kv_heads, group):
    *blocks, out = refs
    rows = q.shape[0]
    scale = 1.0 / math.sqrt(HS)
    allowed = kpos[...] <= qpos[...]
    allowed = jnp.concatenate([allowed] * group, axis=0)
    for g in range(kv_heads):
        k = jnp.concatenate([b[:, g * HS : (g + 1) * HS] for b in blocks], axis=0)
        lo = kv_heads * HS + g * HS
        v = jnp.concatenate([b[:, lo : lo + HS] for b in blocks], axis=0)
        heads = [g * group + j for j in range(group)]
        qs = jnp.concatenate([q[:, h * HS : (h + 1) * HS] for h in heads], axis=0)
        scores = (
            lax.dot_general(qs, k, (((1,), (1,)), ((), ())), preferred_element_type=jnp.float32)
            * scale
        )
        masked = jnp.where(allowed, scores, -1e30)
        best = jnp.max(masked, axis=-1, keepdims=True)
        weights = jnp.where(allowed, jnp.exp(masked - best), 0.0)
        total = jnp.sum(weights, axis=-1, keepdims=True)
        acc = jnp.dot(weights.astype(jnp.bfloat16), v, preferred_element_type=jnp.float32)
        attended = (acc / total).astype(jnp.bfloat16)
        for j, h in enumerate(heads):
            out[:, h * HS : (h + 1) * HS] = attended[j * rows : (j + 1) * rows]


def attend(q, qpos, kpos, blocks):
    rows, q_cols = q.shape
    kv_heads = blocks[0].shape[1] // (2 * HS)
    group = q_cols // HS // kv_heads

    def body(*refs):
        attend_kernel(*refs, kv_heads=kv_heads, group=group)

    keys = sum(b.shape[0] for b in blocks)
    return pl.pallas_call(
        body,
        out_shape=jax.ShapeDtypeStruct((rows, q_cols), jnp.bfloat16),
        compiler_params=pltpu.CompilerParams(vmem_limit_bytes=VMEM),
        cost_estimate=pl.CostEstimate(
            flops=4 * rows * q_cols * keys,
            bytes_accessed=4 * rows * q_cols,
            transcendentals=rows * keys * q_cols // HS,
        ),
        name="attend",
    )(q, qpos, kpos, *blocks)


def out_part(targets, attended, w_out, width, tile, split):
    rows, depth = attended.shape
    per_target = width // tile
    steps = per_target * len(targets)
    n_outs = 2 if split else 1
    half = rows // n_outs

    def body(col_ref, a, w, *outs):
        i = pl.program_id(0)
        part = jnp.dot(a[...], w[0], preferred_element_type=jnp.float32).astype(jnp.bfloat16)
        for n in range(len(targets)):

            @pl.when(i // per_target == n)
            def _():
                at = pl.ds(pl.multiple_of(i % per_target * tile, tile), tile)
                for m in range(n_outs):
                    outs[n * n_outs + m][:, at] = part[m * half : (m + 1) * half]

    cols = jnp.stack(targets).astype(jnp.int32)
    return pl.pallas_call(
        body,
        grid_spec=pltpu.PrefetchScalarGridSpec(
            num_scalar_prefetch=1,
            grid=(steps,),
            in_specs=[
                pl.BlockSpec((rows, depth), lambda i, c: (0, 0)),
                pl.BlockSpec(
                    (1, depth, tile),
                    lambda i, c: (0, 0, c[i // per_target] // tile + i % per_target),
                ),
            ],
            out_specs=[pl.BlockSpec((half, width), lambda i, c: (0, 0))] * n_outs * len(targets),
        ),
        out_shape=[jax.ShapeDtypeStruct((half, width), jnp.bfloat16)] * n_outs * len(targets),
        compiler_params=pltpu.CompilerParams(vmem_limit_bytes=VMEM),
        cost_estimate=pl.CostEstimate(
            flops=2 * rows * depth * width * len(targets),
            bytes_accessed=2 * depth * width * len(targets),
            transcendentals=0,
        ),
        name="out_part",
    )(cols, attended, w_out)


def add_all(x, parts):
    total = parts[0].astype(jnp.float32)
    for p in parts[1:]:
        total = total + p.astype(jnp.float32)
    return (x.astype(jnp.float32) + total).astype(jnp.bfloat16)


def per_device(tokens, norm_gain, wq, wk, wv, w_out):
    n_ctx = lax.axis_size("ctx")
    n_tp = lax.axis_size("tp")
    n_z = n_ctx // 4
    section = lax.axis_index("section")
    ctx = lax.axis_index("ctx")
    tp = lax.axis_index("tp")
    x_lo = ctx // (n_ctx // 2)
    z = (ctx // 2) % n_z
    core = ctx % 2
    half = tokens.shape[1]
    width = tokens.shape[2]
    chunk = width // CHUNKS
    gain = norm_gain.astype(jnp.float32)

    local = lax.iota(jnp.int32, half)

    def positions(z_of, core_of):
        base = (z_of * 2 + core_of) * half + local
        mine = x_lo * (n_ctx // 2) * half + base
        theirs = (1 - x_lo) * (n_ctx // 2) * half + base
        return jnp.concatenate([mine, theirs])

    qpos = positions(z, core)
    z_of = [(z - s) % n_z for s in range(n_z)]
    kpos = jnp.concatenate(
        [positions(zs, core) for zs in z_of] + [positions(zs, 1 - core) for zs in z_of]
    )
    pairs = lax.iota(jnp.int32, HS // 2).astype(jnp.float32)
    freqs = jnp.power(jnp.float32(500000.0), -2.0 * pairs / HS)
    angle = qpos.astype(jnp.float32)[:, None] * freqs[None, :]
    cosine = jnp.cos(angle)
    sine = jnp.sin(angle)
    rope = (
        jnp.concatenate([cosine, cosine], axis=1),
        jnp.concatenate([-sine, sine], axis=1),
    )
    qpos = qpos[:, None]
    kpos = kpos[None, :]
    src = [(tp - s) % n_tp * width for s in range(n_tp)]
    dst = [(tp + s) % n_tp * width for s in range(n_tp)]

    def mix(where, kv, make_q):
        mine = [kv] + [send(kv, where, by_z=s) for s in range(1, n_z)]
        q = make_q()
        theirs = [send(b, where, other_core=True) for b in mine]
        return attend(q, qpos, kpos, mine + theirs)

    own = lax.dynamic_index_in_dim(tokens, x_lo, 0, keepdims=False)
    other = lax.dynamic_index_in_dim(tokens, 1 - x_lo, 0, keepdims=False)
    own_from, other_from = [own], []
    for s in range(n_tp):
        if s:
            own_from.append(send(own, FIRST, by_tp=s))
        other_from.append(send(other, FIRST, by_tp=s, other_half=True))
    pieces = [(src[s], [own_from[s], other_from[s]]) for s in (0, 1, 3, 2)]
    carry = project_kv(pieces[:3], gain, wk, wv, None, None, 512)
    kv, r = project_kv(pieces[3:], gain, wk, wv, carry, rope, 512)
    attended = mix(FIRST, kv, lambda: project_q(pieces, gain, wq, r, rope, 512))

    x0 = jnp.concatenate([own, other_from[0]], axis=0)
    sums = []
    for c in range(CHUNKS):
        at = c * chunk
        parts = []
        (far,) = out_part([dst[2] + at], attended, w_out, chunk, 256, False)
        parts.append(send(far, FIRST, by_tp=2))
        near = out_part([dst[1] + at, dst[3] + at], attended, w_out, chunk, 256, False)
        parts.append(send(near[0], FIRST, by_tp=1))
        parts.append(send(near[1], FIRST, by_tp=3))
        parts.append(out_part([dst[0] + at], attended, w_out, chunk, 256, False)[0])
        sums.append(add_all(x0[:, at : at + chunk], parts))

    received = [send(x, FIRST, to=1) for x in sums]
    carry = None
    pieces = []
    for c in range(CHUNKS):
        got = [received[c]] + [send(received[c], SECOND, by_tp=s) for s in range(1, n_tp)]
        now = [(src[s] + c * chunk, [got[s]]) for s in (0, 1, 3, 2)]
        pieces += now
        carry = project_kv(now, gain, wk, wv, carry, rope if c == CHUNKS - 1 else None, chunk)
    kv, r = carry
    x1 = jnp.concatenate(
        [jnp.where(section == 0, a, b) for a, b in zip(sums, received)], axis=1
    )
    kept_own = x1[:half]
    kept_cross = x1[half:]
    kept_cross = send(kept_cross, BOTH, other_half=True)
    attended = mix(SECOND, kv, lambda: project_q(pieces, gain, wq, r, rope, chunk))
    own_parts, cross_parts = [], []
    for group in ((2,), (1, 3), (0,)):
        outs = out_part([dst[s] for s in group], attended, w_out, width, 256, True)
        for n, s in enumerate(group):
            cross_parts.append(send(outs[2 * n + 1], SECOND, by_tp=s, other_half=True))
            own_parts.append(outs[2 * n] if s == 0 else send(outs[2 * n], SECOND, by_tp=s))
    out_own = jnp.where(section == 0, kept_own, add_all(kept_own, own_parts))
    out_cross = jnp.where(section == 0, kept_cross, add_all(kept_cross, cross_parts))
    first = jnp.where(x_lo == 0, out_own, out_cross)
    second = jnp.where(x_lo == 0, out_cross, out_own)
    return jnp.stack([first, second])[None]


def solution(mesh):
    return jax.shard_map(
        per_device,
        mesh=mesh,
        in_specs=(
            P(None, "ctx", "tp"),
            P("section", None),
            P("section", None, "tp"),
            P("section", None, "tp"),
            P("section", None, "tp"),
            P("section", "tp", None),
        ),
        out_specs=P("section", None, "ctx", "tp"),
        check_vma=False,
    )
```

```python
import itertools
import math
import jax
import jax.numpy as jnp
from jax import lax
from jax.experimental import pallas as pl
from jax.experimental.pallas import tpu as pltpu
from jax.sharding import PartitionSpec as P

HS = 128
EPS = 1e-05
CHUNKS = 2
SMALL = 12 * 1024 * 1024
LARGE = 28 * 1024 * 1024
SHIFTS = (2, 1, 3, 0)
AXES = ("section", "ctx", "tp")


def send(block, by_tp=0, by_z=0, other_half=False, other_core=False, next_layer=False):
    n_section = lax.axis_size("section")
    n_ctx = lax.axis_size("ctx")
    n_tp = lax.axis_size("tp")
    n_half = n_ctx // 2
    route = []
    for e, c, t in itertools.product(range(n_section), range(n_ctx), range(n_tp)):
        there = (c % n_half + 2 * by_z) % n_half + c // n_half * n_half
        if other_half or next_layer:
            there = (there + n_half) % n_ctx
        if other_core:
            there = there ^ 1
        end = (e + next_layer) % n_section
        route.append(
            ((e * n_ctx + c) * n_tp + t, (end * n_ctx + there) * n_tp + (t + by_tp) % n_tp)
        )
    return lax.ppermute(block, AXES, route)


def in_vmem(kernel, operands, out_shape, name, in_hbm=(), scratch=(), limit=None, flops=0):
    n_bytes = sum(x.size * x.dtype.itemsize for x in (*operands, *in_hbm))
    specs = [pl.BlockSpec(memory_space=pltpu.VMEM)] * len(operands)
    specs += [pl.BlockSpec(memory_space=pl.ANY)] * len(in_hbm)
    return pl.pallas_call(
        kernel,
        in_specs=specs,
        out_specs=[pl.BlockSpec(memory_space=pltpu.VMEM)] * len(out_shape),
        out_shape=[jax.ShapeDtypeStruct(shape, dtype) for shape, dtype in out_shape],
        scratch_shapes=list(scratch),
        compiler_params=pltpu.CompilerParams(vmem_limit_bytes=limit or SMALL),
        cost_estimate=pl.CostEstimate(flops=flops, bytes_accessed=n_bytes, transcendentals=0),
        name=name,
    )(*operands, *[pltpu.with_memory_space_constraint(w, pltpu.HBM) for w in in_hbm])


def from_slice(shift, at, width):
    n_tp = lax.axis_size("tp")
    tp = lax.axis_index("tp")
    return pl.multiple_of(lax.rem(tp + (n_tp - shift) % n_tp, n_tp) * width + at, HS)


def scaled_piece(rows_of, gain, start):
    x = jnp.concatenate([r[...] for r in rows_of], axis=0).astype(jnp.float32)
    g = gain[:, pl.ds(start, x.shape[1])]
    return (x * g).astype(jnp.bfloat16), jnp.sum(x * x, axis=-1, keepdims=True)


def rotated(u, cos, sin):
    return u * cos + pltpu.roll(u, HS // 2, 1) * sin


def flat_pieces(pieces):
    return [r for _, _, rows_of in pieces for r in rows_of]


def regroup(refs, pieces):
    out, at = [], 0
    for _, _, rows_of in pieces:
        out.append(refs[at : at + len(rows_of)])
        at += len(rows_of)
    return out, refs[at:]


def project_kv(pieces, slice_width, gain, weights, carry, rope, following):
    rows = sum(x.shape[0] for x in pieces[0][2])
    width = pieces[0][2][0].shape[1]
    kv_cols = weights[0].shape[-1]
    n = len(pieces)
    first, last = carry is None, rope is not None
    n_next = len(following)

    def body(*refs):
        groups, refs = regroup(refs, pieces)
        gain_ref = refs[0]
        refs = refs[1:]
        if not first:
            acc_in, ss_in = refs[:2]
            refs = refs[2:]
        if last:
            cos, sin = refs[:2]
            refs = refs[2:]
        w_refs = refs[:2]
        refs = refs[2:]
        copies = []
        if n_next:
            outs, next_refs, (held_k, held_v, sems) = refs[:2], refs[2:4], refs[4:]
            for j, (shift, at, *_) in enumerate(list(pieces) + list(following)):
                there = pl.ds(from_slice(shift, at, slice_width), width)
                to = pl.ds((j if j < n else j - n) * width, width)
                for m in range(2):
                    hold = (held_k, held_v)[m] if j < n else next_refs[m]
                    copies.append(
                        pltpu.make_async_copy(
                            w_refs[m].at[0, there, :], hold.at[to, :], sems.at[j, m]
                        )
                    )
            for c in copies:
                c.start()
            w_refs = (held_k, held_v)
        else:
            outs = refs
        ss = k = v = None
        if not first:
            ss, k, v = ss_in[...], acc_in[:, :kv_cols], acc_in[:, kv_cols:]
        for j, ((shift, at, _), rows_of) in enumerate(zip(pieces, groups)):
            start = from_slice(shift, at, slice_width)
            x, squares = scaled_piece(rows_of, gain_ref, start)
            here = slice(j * width, (j + 1) * width)
            if copies:
                copies[2 * j].wait()
            pk = jnp.dot(x, w_refs[0][here, :], preferred_element_type=jnp.float32)
            if copies:
                copies[2 * j + 1].wait()
            pv = jnp.dot(x, w_refs[1][here, :], preferred_element_type=jnp.float32)
            ss = squares if ss is None else ss + squares
            k = pk if k is None else k + pk
            v = pv if v is None else v + pv
        if last:
            out, r_out = outs
            r = lax.rsqrt(ss / 4096.0 + EPS)
            r_out[...] = r
            for h in range(kv_cols // HS):
                at = slice(h * HS, (h + 1) * HS)
                out[:, at] = rotated(k[:, at] * r, cos[...], sin[...]).astype(jnp.bfloat16)
            out[:, kv_cols:] = (v * r).astype(jnp.bfloat16)
        else:
            acc, ss_out = outs
            acc[:, :kv_cols] = k
            acc[:, kv_cols:] = v
            ss_out[...] = ss
        for c in copies[2 * n :]:
            c.wait()

    operands = flat_pieces(pieces) + [gain]
    operands += [] if first else list(carry)
    operands += list(rope) if last else []
    kind = jnp.bfloat16 if last else jnp.float32
    out_shape = [((rows, 2 * kv_cols), kind), ((rows, 1), jnp.float32)]
    scratch = []
    if n_next:
        out_shape += [((n_next * width, kv_cols), jnp.bfloat16)] * 2
        scratch = [pltpu.VMEM((n * width, kv_cols), jnp.bfloat16)] * 2
        scratch.append(pltpu.SemaphoreType.DMA((n + n_next, 2)))
    else:
        operands += list(weights)
    got = in_vmem(
        body,
        operands,
        out_shape,
        "project_kv",
        in_hbm=weights if n_next else (),
        scratch=scratch,
        flops=4 * rows * n * width * kv_cols,
    )
    return got[:2], got[2:]


def project_q(pieces, slice_width, gain, wq, r, rope):
    rows = sum(x.shape[0] for x in pieces[0][2])
    width = pieces[0][2][0].shape[1]
    cols = wq.shape[2]
    n = len(pieces)

    def body(*refs):
        groups, refs = regroup(refs, pieces)
        gain_ref, r_ref, cos, sin, w_ref, out, held, sems = refs
        starts = [from_slice(shift, at, slice_width) for shift, at, _ in pieces]
        copies = [
            pltpu.make_async_copy(w_ref.at[0, pl.ds(start, width), :], held.at[j], sems.at[j])
            for j, start in enumerate(starts)
        ]
        for c in copies:
            c.start()
        acc = None
        for j, rows_of in enumerate(groups):
            x, _ = scaled_piece(rows_of, gain_ref, starts[j])
            copies[j].wait()
            part = jnp.dot(x, held[j], preferred_element_type=jnp.float32)
            acc = part if acc is None else acc + part
        for h in range(cols // HS):
            at = slice(h * HS, (h + 1) * HS)
            out[:, at] = rotated(acc[:, at] * r_ref[...], cos[...], sin[...]).astype(
                jnp.bfloat16
            )

    return in_vmem(
        body,
        flat_pieces(pieces) + [gain, r, *rope],
        [((rows, cols), jnp.bfloat16)],
        "project_q",
        in_hbm=[wq],
        scratch=[
            pltpu.VMEM((n, width, cols), jnp.bfloat16),
            pltpu.SemaphoreType.DMA((n,)),
        ],
        limit=LARGE,
        flops=2 * rows * wq.size,
    )[0]


def attend_and_project(q, qpos, kpos, blocks, w_out, chunks, split):
    rows, q_cols = q.shape
    kv_heads = blocks[0].shape[1] // (2 * HS)
    group = q_cols // HS // kv_heads
    scale = 1.0 / math.sqrt(HS)
    n_blocks = len(blocks)
    keys = sum(b.shape[0] for b in blocks)
    _, depth, out_cols = w_out.shape
    slice_width = out_cols // len(SHIFTS)
    width = slice_width // chunks
    parts = [(c, s) for c in range(chunks) for s in SHIFTS]
    n_cut = 2 if split else 1
    half = rows // n_cut

    def body(q, qpos, kpos, *refs):
        block_refs, refs = refs[:n_blocks], refs[n_blocks:]
        w_ref, refs = refs[0], refs[1:]
        outs, (attended, held, sems) = refs[:-3], refs[-3:]
        copies = []
        for j, (c, s) in enumerate(parts):
            there = pl.ds(from_slice(-s, c * width, slice_width), width)
            copies.append(pltpu.make_async_copy(w_ref.at[0, :, there], held.at[j], sems.at[j]))
        for c in copies:
            c.start()
        allowed = kpos[...] <= qpos[...]
        allowed = jnp.concatenate([allowed] * group, axis=0)
        for g in range(kv_heads):
            k = jnp.concatenate([b[:, g * HS : (g + 1) * HS] for b in block_refs], axis=0)
            lo = kv_heads * HS + g * HS
            v = jnp.concatenate([b[:, lo : lo + HS] for b in block_refs], axis=0)
            heads = [g * group + j for j in range(group)]
            qs = jnp.concatenate([q[:, h * HS : (h + 1) * HS] for h in heads], axis=0)
            scores = lax.dot_general(
                qs, k, (((1,), (1,)), ((), ())), preferred_element_type=jnp.float32
            )
            masked = jnp.where(allowed, scores * scale, -1e30)
            best = jnp.max(masked, axis=-1, keepdims=True)
            weights = jnp.where(allowed, jnp.exp(masked - best), 0.0)
            total = jnp.sum(weights, axis=-1, keepdims=True)
            acc = jnp.dot(weights.astype(jnp.bfloat16), v, preferred_element_type=jnp.float32)
            normal = (acc / total).astype(jnp.bfloat16)
            for j, h in enumerate(heads):
                attended[:, h * HS : (h + 1) * HS] = normal[j * rows : (j + 1) * rows]
        for j in range(len(parts)):
            copies[j].wait()
            part = jnp.dot(attended[...], held[j], preferred_element_type=jnp.float32).astype(
                jnp.bfloat16
            )
            for m in range(n_cut):
                outs[j * n_cut + m][...] = part[m * half : (m + 1) * half]

    got = in_vmem(
        body,
        [q, qpos, kpos, *blocks],
        [((half, width), jnp.bfloat16)] * len(parts) * n_cut,
        "attend_and_project",
        in_hbm=[w_out],
        scratch=[
            pltpu.VMEM((rows, q_cols), jnp.bfloat16),
            pltpu.VMEM((len(parts), depth, width), jnp.bfloat16),
            pltpu.SemaphoreType.DMA((len(parts),)),
        ],
        limit=LARGE,
        flops=4 * rows * q_cols * keys + 2 * rows * w_out.size,
    )
    return [got[j * n_cut : (j + 1) * n_cut] for j in range(len(parts))]


def add_all(x, parts):
    total = parts[0].astype(jnp.float32)
    for p in parts[1:]:
        total = total + p.astype(jnp.float32)
    return (x.astype(jnp.float32) + total).astype(jnp.bfloat16)


def per_device(tokens, norm_gain, wq, wk, wv, w_out):
    n_ctx = lax.axis_size("ctx")
    n_tp = lax.axis_size("tp")
    n_z = n_ctx // 4
    section = lax.axis_index("section")
    ctx = lax.axis_index("ctx")
    x_lo = ctx // (n_ctx // 2)
    z = (ctx // 2) % n_z
    core = ctx % 2
    half = tokens.shape[1]
    width = tokens.shape[2]
    chunk = width // CHUNKS
    gain = norm_gain.astype(jnp.float32)

    local = lax.iota(jnp.int32, half)

    def positions(z_of, core_of):
        base = (z_of * 2 + core_of) * half + local
        mine = x_lo * (n_ctx // 2) * half + base
        theirs = (1 - x_lo) * (n_ctx // 2) * half + base
        return jnp.concatenate([mine, theirs])

    z_of = [(z - s) % n_z for s in range(n_z)]
    qpos = positions(z, core)
    kpos = jnp.concatenate(
        [positions(zs, core) for zs in z_of] + [positions(zs, 1 - core) for zs in z_of]
    )

    def tables(qpos):
        pairs = lax.iota(jnp.int32, HS // 2).astype(jnp.float32)
        freqs = jnp.power(jnp.float32(500000.0), -2.0 * pairs / HS)
        angle = qpos.astype(jnp.float32)[:, None] * freqs[None, :]
        cosine = jnp.cos(angle)
        sine = jnp.sin(angle)
        return (
            jnp.concatenate([cosine, cosine], axis=1),
            jnp.concatenate([-sine, sine], axis=1),
        )

    def swapped(rows):
        return jnp.concatenate([rows[half : 2 * half], rows[:half]], axis=0)

    rope = tables(qpos)

    def mix(kv, make_q, qpos, kpos, chunks, split):
        mine = [kv] + [send(kv, by_z=s) for s in (2, 1, 3)]
        q = make_q()
        theirs = [send(b, other_core=True) for b in mine]
        mine = [mine[0], mine[2], mine[1], mine[3]]
        theirs = [theirs[0], theirs[2], theirs[1], theirs[3]]
        return attend_and_project(
            q, qpos[:, None], kpos[None, :], mine + theirs, w_out, chunks, split
        )

    own = lax.dynamic_index_in_dim(tokens, x_lo, 0, keepdims=False)
    other = lax.dynamic_index_in_dim(tokens, 1 - x_lo, 0, keepdims=False)
    own_from, other_from = [own], []
    for s in range(n_tp):
        if s:
            own_from.append(send(own, by_tp=s))
        other_from.append(send(other, by_tp=s, other_half=True))
    pieces = [(s, 0, [own_from[s], other_from[s]]) for s in (0, 1, 3, 2)]
    carry, held = project_kv(pieces[:3], width, gain, (wk, wv), None, None, pieces[3:])
    (kv, r), _ = project_kv(pieces[3:], width, gain, held, carry, rope, ())
    got = mix(
        kv, lambda: project_q(pieces, width, gain, wq, r, rope), qpos, kpos, CHUNKS, False
    )
    x0 = jnp.concatenate([own, other_from[0]], axis=0)
    sums = []
    for c in range(CHUNKS):
        at = c * chunk
        parts = []
        for s, (block,) in zip(SHIFTS, got[c * n_tp : (c + 1) * n_tp]):
            parts.append(send(block, by_tp=s) if s else block)
        sums.append(add_all(x0[:, at : at + chunk], parts))

    received = [send(x, next_layer=True) for x in sums]
    qpos = swapped(qpos)
    kpos = swapped(kpos.reshape(-1, 2 * half).T).T.reshape(-1)
    rope = tuple(swapped(t) for t in rope)
    carry, held = None, (wk, wv)
    pieces = []
    for c in range(CHUNKS):
        got = [received[c]] + [send(received[c], by_tp=s) for s in (2, 1, 3)]
        pieces.append([(s, c * chunk, [g]) for s, g in zip((0, 2, 1, 3), got)])
    for c in range(CHUNKS):
        last = c == CHUNKS - 1
        following = () if last else pieces[c + 1]
        carry, held = project_kv(
            pieces[c], width, gain, held, carry, rope if last else None, following
        )
    kv, r = carry
    x1 = jnp.concatenate(sums, axis=1)
    came = jnp.concatenate(received, axis=1)
    kept_own = jnp.where(section == 0, x1[:half], came[half:])
    kept_cross = send(jnp.where(section == 0, x1[half:], came[:half]), other_half=True)
    every = [p for group in pieces for p in group]
    got = mix(kv, lambda: project_q(every, width, gain, wq, r, rope), qpos, kpos, 1, True)
    own_parts, cross_parts = [], []
    for s, (theirs, mine) in zip(SHIFTS, got):
        cross_parts.append(send(theirs, by_tp=s, other_half=True))
        own_parts.append(send(mine, by_tp=s) if s else mine)
    out_own = jnp.where(section == 0, kept_own, add_all(kept_own, own_parts))
    out_cross = jnp.where(section == 0, kept_cross, add_all(kept_cross, cross_parts))
    own_first = x_lo == section
    first = jnp.where(own_first, out_own, out_cross)
    second = jnp.where(own_first, out_cross, out_own)
    return jnp.stack([first, second])[None]


def solution(mesh):
    return jax.shard_map(
        per_device,
        mesh=mesh,
        in_specs=(
            P(None, "ctx", "tp"),
            P("section", None),
            P("section", None, "tp"),
            P("section", None, "tp"),
            P("section", None, "tp"),
            P("section", "tp", None),
        ),
        out_specs=P("section", None, "ctx", "tp"),
        check_vma=False,
    )
```

```python
import itertools
import math
import jax
import jax.numpy as jnp
from jax import lax
from jax.experimental import pallas as pl
from jax.experimental.pallas import tpu as pltpu
from jax.sharding import PartitionSpec as P

HS = 128
EPS = 1e-05
CHUNKS = 2
SMALL = 12 * 1024 * 1024
LARGE = 28 * 1024 * 1024
SHIFTS = (2, 1, 3, 0)
AXES = ("section", "ctx", "tp")


def send(block, by_tp=0, by_z=0, other_half=False, other_core=False, next_layer=False):
    n_section = lax.axis_size("section")
    n_ctx = lax.axis_size("ctx")
    n_tp = lax.axis_size("tp")
    n_half = n_ctx // 2
    route = []
    for e, c, t in itertools.product(range(n_section), range(n_ctx), range(n_tp)):
        there = (c % n_half + 2 * by_z) % n_half + c // n_half * n_half
        if other_half or next_layer:
            there = (there + n_half) % n_ctx
        if other_core:
            there = there ^ 1
        end = (e + next_layer) % n_section
        route.append(
            ((e * n_ctx + c) * n_tp + t, (end * n_ctx + there) * n_tp + (t + by_tp) % n_tp)
        )
    return lax.ppermute(block, AXES, route)


def in_vmem(kernel, operands, out_shape, name, in_hbm=(), scratch=(), limit=None, flops=0):
    n_bytes = sum(x.size * x.dtype.itemsize for x in (*operands, *in_hbm))
    specs = [pl.BlockSpec(memory_space=pltpu.VMEM)] * len(operands)
    specs += [pl.BlockSpec(memory_space=pl.ANY)] * len(in_hbm)
    return pl.pallas_call(
        kernel,
        in_specs=specs,
        out_specs=[pl.BlockSpec(memory_space=pltpu.VMEM)] * len(out_shape),
        out_shape=[jax.ShapeDtypeStruct(shape, dtype) for shape, dtype in out_shape],
        scratch_shapes=list(scratch),
        compiler_params=pltpu.CompilerParams(vmem_limit_bytes=limit or SMALL),
        cost_estimate=pl.CostEstimate(flops=flops, bytes_accessed=n_bytes, transcendentals=0),
        name=name,
    )(*operands, *[pltpu.with_memory_space_constraint(w, pltpu.HBM) for w in in_hbm])


def from_slice(shift, at, width):
    n_tp = lax.axis_size("tp")
    tp = lax.axis_index("tp")
    return pl.multiple_of(lax.rem(tp + (n_tp - shift) % n_tp, n_tp) * width + at, HS)


def scaled_piece(rows_of, gain, start):
    x = jnp.concatenate([r[...] for r in rows_of], axis=0).astype(jnp.float32)
    g = gain[:, pl.ds(start, x.shape[1])]
    return (x * g).astype(jnp.bfloat16), jnp.sum(x * x, axis=-1, keepdims=True)


def rotated(u, cos, sin):
    return u * cos + pltpu.roll(u, HS // 2, 1) * sin


def flat_pieces(pieces):
    return [r for _, _, rows_of in pieces for r in rows_of]


def regroup(refs, pieces):
    out, at = [], 0
    for _, _, rows_of in pieces:
        out.append(refs[at : at + len(rows_of)])
        at += len(rows_of)
    return out, refs[at:]


def bring(after, *weights):
    def body(after_ref, *refs):
        n = len(weights)
        sems = refs[-1]
        copies = [
            pltpu.make_async_copy(refs[i].at[0], refs[n + i], sems.at[i]) for i in range(n)
        ]
        for c in copies:
            c.start()
        for c in copies:
            c.wait()

    return in_vmem(
        body,
        [after],
        [(w.shape[1:], w.dtype) for w in weights],
        "bring",
        in_hbm=weights,
        scratch=[pltpu.SemaphoreType.DMA((len(weights),))],
    )


def project_kv(pieces, slice_width, gain, weights, carry, rope, following):
    rows = sum(x.shape[0] for x in pieces[0][2])
    width = pieces[0][2][0].shape[1]
    kv_cols = weights[0].shape[-1]
    n = len(pieces)
    first, last = carry is None, rope is not None
    n_next = len(following)
    whole = not n_next and weights[0].shape[0] > n * width

    def body(*refs):
        groups, refs = regroup(refs, pieces)
        gain_ref = refs[0]
        refs = refs[1:]
        if not first:
            acc_in, ss_in = refs[:2]
            refs = refs[2:]
        if last:
            cos, sin = refs[:2]
            refs = refs[2:]
        w_refs = refs[:2]
        refs = refs[2:]
        copies = []
        if n_next:
            outs, next_refs, (held_k, held_v, sems) = refs[:2], refs[2:4], refs[4:]
            for j, (shift, at, *_) in enumerate(list(pieces) + list(following)):
                there = pl.ds(from_slice(shift, at, slice_width), width)
                to = pl.ds((j if j < n else j - n) * width, width)
                for m in range(2):
                    hold = (held_k, held_v)[m] if j < n else next_refs[m]
                    copies.append(
                        pltpu.make_async_copy(
                            w_refs[m].at[0, there, :], hold.at[to, :], sems.at[j, m]
                        )
                    )
            for c in copies:
                c.start()
            w_refs = (held_k, held_v)
        else:
            outs = refs
        ss = k = v = None
        if not first:
            ss, k, v = ss_in[...], acc_in[:, :kv_cols], acc_in[:, kv_cols:]
        for j, ((shift, at, _), rows_of) in enumerate(zip(pieces, groups)):
            start = from_slice(shift, at, slice_width)
            x, squares = scaled_piece(rows_of, gain_ref, start)
            here = pl.ds(start, width) if whole else slice(j * width, (j + 1) * width)
            if copies:
                copies[2 * j].wait()
            pk = jnp.dot(x, w_refs[0][here, :], preferred_element_type=jnp.float32)
            if copies:
                copies[2 * j + 1].wait()
            pv = jnp.dot(x, w_refs[1][here, :], preferred_element_type=jnp.float32)
            ss = squares if ss is None else ss + squares
            k = pk if k is None else k + pk
            v = pv if v is None else v + pv
        if last:
            out, r_out = outs
            r = lax.rsqrt(ss / 4096.0 + EPS)
            r_out[...] = r
            for h in range(kv_cols // HS):
                at = slice(h * HS, (h + 1) * HS)
                out[:, at] = rotated(k[:, at] * r, cos[...], sin[...]).astype(jnp.bfloat16)
            out[:, kv_cols:] = (v * r).astype(jnp.bfloat16)
        else:
            acc, ss_out = outs
            acc[:, :kv_cols] = k
            acc[:, kv_cols:] = v
            ss_out[...] = ss
        for c in copies[2 * n :]:
            c.wait()

    operands = flat_pieces(pieces) + [gain]
    operands += [] if first else list(carry)
    operands += list(rope) if last else []
    kind = jnp.bfloat16 if last else jnp.float32
    out_shape = [((rows, 2 * kv_cols), kind), ((rows, 1), jnp.float32)]
    scratch = []
    if n_next:
        out_shape += [((n_next * width, kv_cols), jnp.bfloat16)] * 2
        scratch = [pltpu.VMEM((n * width, kv_cols), jnp.bfloat16)] * 2
        scratch.append(pltpu.SemaphoreType.DMA((n + n_next, 2)))
    else:
        operands += list(weights)
    got = in_vmem(
        body,
        operands,
        out_shape,
        "project_kv",
        in_hbm=weights if n_next else (),
        scratch=scratch,
        flops=4 * rows * n * width * kv_cols,
    )
    return got[:2], got[2:]


def project_q(pieces, slice_width, gain, wq, r, rope):
    rows = sum(x.shape[0] for x in pieces[0][2])
    width = pieces[0][2][0].shape[1]
    cols = wq.shape[2]
    n = len(pieces)

    def body(*refs):
        groups, refs = regroup(refs, pieces)
        gain_ref, r_ref, cos, sin, w_ref, out, held, sems = refs
        starts = [from_slice(shift, at, slice_width) for shift, at, _ in pieces]
        copies = [
            pltpu.make_async_copy(w_ref.at[0, pl.ds(start, width), :], held.at[j], sems.at[j])
            for j, start in enumerate(starts)
        ]
        for c in copies:
            c.start()
        acc = None
        for j, rows_of in enumerate(groups):
            x, _ = scaled_piece(rows_of, gain_ref, starts[j])
            copies[j].wait()
            part = jnp.dot(x, held[j], preferred_element_type=jnp.float32)
            acc = part if acc is None else acc + part
        r = r_ref[...] * (math.log2(math.e) / math.sqrt(HS))
        for h in range(cols // HS):
            at = slice(h * HS, (h + 1) * HS)
            out[:, at] = rotated(acc[:, at] * r, cos[...], sin[...]).astype(jnp.bfloat16)

    return in_vmem(
        body,
        flat_pieces(pieces) + [gain, r, *rope],
        [((rows, cols), jnp.bfloat16)],
        "project_q",
        in_hbm=[wq],
        scratch=[
            pltpu.VMEM((n, width, cols), jnp.bfloat16),
            pltpu.SemaphoreType.DMA((n,)),
        ],
        limit=LARGE,
        flops=2 * rows * wq.size,
    )[0]


def attend_and_project(q, qpos, kpos, blocks, w_out, width, split, now, later):
    rows, q_cols = q.shape
    kv_heads = blocks[0].shape[1] // (2 * HS)
    group = q_cols // HS // kv_heads
    n_blocks = len(blocks)
    keys = sum(b.shape[0] for b in blocks)
    _, depth, out_cols = w_out.shape
    slice_width = out_cols // lax.axis_size("tp")
    n_cut = 2 if split else 1
    half = rows // n_cut
    n_now, n_later = len(now), len(later)

    def body(q, qpos, kpos, *refs):
        block_refs, refs = refs[:n_blocks], refs[n_blocks:]
        w_ref, refs = refs[0], refs[1:]
        outs, refs = refs[: n_now * n_cut], refs[n_now * n_cut :]
        attended, later_ref, held, sems = refs
        copies = []
        for j, (at, s) in enumerate(list(now) + list(later)):
            there = pl.ds(from_slice(-s, at, slice_width), width)
            to = held.at[j] if j < n_now else later_ref.at[j - n_now]
            copies.append(pltpu.make_async_copy(w_ref.at[0, :, there], to, sems.at[j]))
        for c in copies:
            c.start()
        bias = jnp.where(kpos[...] <= qpos[...], 0.0, -1e30)
        ones = jnp.ones((keys, HS), jnp.bfloat16)
        for g in range(kv_heads):
            k = jnp.concatenate([b[:, g * HS : (g + 1) * HS] for b in block_refs], axis=0)
            lo = kv_heads * HS + g * HS
            v = jnp.concatenate([b[:, lo : lo + HS] for b in block_refs], axis=0)
            v = jnp.concatenate([v, ones], axis=1)
            heads = [g * group + j for j in range(group)]
            qs = jnp.concatenate([q[:, h * HS : (h + 1) * HS] for h in heads], axis=0)
            scores = lax.dot_general(
                qs, k, (((1,), (1,)), ((), ())), preferred_element_type=jnp.float32
            )
            scores = scores.reshape(group, rows, keys) + bias[None]
            best = jnp.max(scores, axis=-1, keepdims=True)
            weights = jnp.exp2(scores - best).astype(jnp.bfloat16).reshape(group * rows, keys)
            acc = jnp.dot(weights, v, preferred_element_type=jnp.float32)
            normal = (acc[:, :HS] / acc[:, HS:]).astype(jnp.bfloat16)
            for j, h in enumerate(heads):
                attended[:, h * HS : (h + 1) * HS] = normal[j * rows : (j + 1) * rows]
        for j in range(n_now):
            copies[j].wait()
            part = jnp.dot(attended[...], held[j], preferred_element_type=jnp.float32).astype(
                jnp.bfloat16
            )
            for m in range(n_cut):
                outs[j * n_cut + m][...] = part[m * half : (m + 1) * half]
        for c in copies[n_now:]:
            c.wait()

    got = in_vmem(
        body,
        [q, qpos, kpos, *blocks],
        [((half, width), jnp.bfloat16)] * n_now * n_cut
        + [((rows, q_cols), jnp.bfloat16), ((n_later, depth, width), jnp.bfloat16)],
        "attend_and_project",
        in_hbm=[w_out],
        scratch=[
            pltpu.VMEM((n_now, depth, width), jnp.bfloat16),
            pltpu.SemaphoreType.DMA((n_now + n_later,)),
        ],
        limit=LARGE,
        flops=4 * rows * q_cols * keys + 2 * rows * w_out.size,
    )
    parts = [got[j * n_cut : (j + 1) * n_cut] for j in range(n_now)]
    return parts, got[-2], got[-1]


def project_out(attended, weights, split):
    rows, depth = attended.shape
    n, _, width = weights.shape
    n_cut = 2 if split else 1
    half = rows // n_cut

    def body(a, w, *outs):
        for j in range(n):
            part = jnp.dot(a[...], w[j], preferred_element_type=jnp.float32).astype(
                jnp.bfloat16
            )
            for m in range(n_cut):
                outs[j * n_cut + m][...] = part[m * half : (m + 1) * half]

    got = in_vmem(
        body,
        [attended, weights],
        [((half, width), jnp.bfloat16)] * n * n_cut,
        "project_out",
        flops=2 * rows * depth * width * n,
    )
    return [got[j * n_cut : (j + 1) * n_cut] for j in range(n)]


def total_of(parts):
    total = parts[0][...].astype(jnp.float32)
    for p in parts[1:]:
        total = total + p[...].astype(jnp.float32)
    return total


def add_parts(x_rows, at, parts):
    rows, width = parts[0].shape
    n = len(x_rows)

    def body(*refs):
        x = jnp.concatenate([r[:, at : at + width] for r in refs[:n]], axis=0)
        out = refs[-1]
        out[...] = (x.astype(jnp.float32) + total_of(refs[n:-1])).astype(jnp.bfloat16)

    return in_vmem(body, [*x_rows, *parts], [((rows, width), jnp.bfloat16)], "add_parts")[0]


def finish(kept_own, own_parts, kept_cross, cross_parts):
    half, width = kept_own.shape
    n_own, n_cross = len(own_parts), len(cross_parts)
    n_half = lax.axis_size("ctx") // 2

    def body(*refs):
        ko, kc, refs = refs[0], refs[1], refs[2:]
        out = refs[-1]
        section = lax.axis_index("section")
        x_lo = lax.axis_index("ctx") // n_half
        first = section == 0
        own = ko[...].astype(jnp.float32) + jnp.where(first, 0.0, total_of(refs[:n_own]))
        cross = kc[...].astype(jnp.float32) + jnp.where(first, 0.0, total_of(refs[n_own:-1]))
        own_first = x_lo == section
        out[0, 0] = jnp.where(own_first, own, cross).astype(jnp.bfloat16)
        out[0, 1] = jnp.where(own_first, cross, own).astype(jnp.bfloat16)

    return in_vmem(
        body,
        [kept_own, kept_cross, *own_parts, *cross_parts],
        [((1, 2, half, width), jnp.bfloat16)],
        "finish",
    )[0]


def per_device(tokens, norm_gain, wq, wk, wv, w_out):
    n_ctx = lax.axis_size("ctx")
    n_tp = lax.axis_size("tp")
    n_z = n_ctx // 4
    section = lax.axis_index("section")
    ctx = lax.axis_index("ctx")
    x_lo = ctx // (n_ctx // 2)
    z = (ctx // 2) % n_z
    core = ctx % 2
    half = tokens.shape[1]
    width = tokens.shape[2]
    chunk = width // CHUNKS
    gain = norm_gain.astype(jnp.float32)

    local = lax.iota(jnp.int32, half)

    def positions(z_of, core_of):
        base = (z_of * 2 + core_of) * half + local
        mine = x_lo * (n_ctx // 2) * half + base
        theirs = (1 - x_lo) * (n_ctx // 2) * half + base
        return jnp.concatenate([mine, theirs])

    z_of = [(z - s) % n_z for s in range(n_z)]
    qpos = positions(z, core)
    kpos = jnp.concatenate(
        [positions(zs, core) for zs in z_of] + [positions(zs, 1 - core) for zs in z_of]
    )

    def tables(qpos):
        pairs = lax.iota(jnp.int32, HS // 2).astype(jnp.float32)
        freqs = jnp.power(jnp.float32(500000.0), -2.0 * pairs / HS)
        angle = qpos.astype(jnp.float32)[:, None] * freqs[None, :]
        cosine = jnp.cos(angle)
        sine = jnp.sin(angle)
        return (
            jnp.concatenate([cosine, cosine], axis=1),
            jnp.concatenate([-sine, sine], axis=1),
        )

    def swapped(rows):
        return jnp.concatenate([rows[half : 2 * half], rows[:half]], axis=0)

    rope = tables(qpos)

    def mix(kv, make_q, qpos, kpos, width, split, now, later):
        theirs = [send(kv, other_core=True)]
        mine = [send(kv, by_z=s) for s in (2, 1, 3)]
        q, *mine = lax.optimization_barrier((make_q(), *mine))
        theirs += [send(mine[n], other_core=True) for n in (1, 0, 2)]
        mine = [kv, mine[1], mine[0], mine[2]]
        return attend_and_project(
            q, qpos[:, None], kpos[None, :], mine + theirs, w_out, width, split, now, later
        )

    own = lax.dynamic_index_in_dim(tokens, x_lo, 0, keepdims=False)
    other = lax.dynamic_index_in_dim(tokens, 1 - x_lo, 0, keepdims=False)
    own_from, other_from = {0: own}, {}
    for s in (2, 1, 3, 0):
        if s:
            own_from[s] = send(own, by_tp=s)
        other_from[s] = send(other, by_tp=s, other_half=True)
    pieces = [(s, 0, [own_from[s], other_from[s]]) for s in (0, 1, 3, 2)]
    carry, held = project_kv(pieces[:3], width, gain, (wk, wv), None, None, pieces[3:])
    (kv, r), _ = project_kv(pieces[3:], width, gain, held, carry, rope, ())
    chunked = [[(c * chunk, s) for s in SHIFTS] for c in range(CHUNKS)]
    got, attended, held = mix(
        kv,
        lambda: project_q(pieces, width, gain, wq, r, rope),
        qpos,
        kpos,
        chunk,
        False,
        chunked[0],
        sum(chunked[1:], []),
    )
    got += project_out(attended, held, False)
    sums = []
    for c in range(CHUNKS):
        parts = []
        for s, (block,) in zip(SHIFTS, got[c * n_tp : (c + 1) * n_tp]):
            parts.append(send(block, by_tp=s) if s else block)
        sums.append(add_parts([own, other_from[0]], c * chunk, parts))

    received = [send(x, next_layer=True) for x in sums]
    qpos = swapped(qpos)
    kpos = swapped(kpos.reshape(-1, 2 * half).T).T.reshape(-1)
    rope = tuple(swapped(t) for t in rope)
    near = bring(sums[-1][:8, :HS], wk, wv)
    carry = None
    pieces = []
    for c in range(CHUNKS):
        came = {0: received[c]}
        for s in (2, 1, 3):
            came[s] = send(received[c], by_tp=s)
        pieces.append([(s, c * chunk, [came[s]]) for s in (0, 1, 3, 2)])
    for c in range(CHUNKS):
        last = c == CHUNKS - 1
        carry, _ = project_kv(pieces[c], width, gain, near, carry, rope if last else None, ())
    kv, r = carry
    x1 = jnp.concatenate(sums, axis=1)
    came = jnp.concatenate(received, axis=1)
    kept_own = jnp.where(section == 0, x1[:half], came[half:])
    kept_cross = send(jnp.where(section == 0, x1[half:], came[:half]), other_half=True)
    every = [p for group in pieces for p in group]
    got, attended, held = mix(
        kv,
        lambda: project_q(every, width, gain, wq, r, rope),
        qpos,
        kpos,
        width,
        True,
        [(0, 2)],
        [(0, s) for s in (1, 3, 0)],
    )
    got += project_out(attended, held, True)
    own_parts, cross_parts = [], []
    for s, (theirs, mine) in zip(SHIFTS, got):
        cross_parts.append(send(theirs, by_tp=s, other_half=True))
        own_parts.append(send(mine, by_tp=s) if s else mine)
    return finish(kept_own, own_parts, kept_cross, cross_parts)


def solution(mesh):
    return jax.shard_map(
        per_device,
        mesh=mesh,
        in_specs=(
            P(None, "ctx", "tp"),
            P("section", None),
            P("section", None, "tp"),
            P("section", None, "tp"),
            P("section", None, "tp"),
            P("section", "tp", None),
        ),
        out_specs=P("section", None, "ctx", "tp"),
        check_vma=False,
    )
```

```python
import itertools
import math
import jax
import jax.numpy as jnp
from jax import lax
from jax.experimental import pallas as pl
from jax.experimental.pallas import tpu as pltpu
from jax.sharding import PartitionSpec as P

HS = 128
EPS = 1e-05
CHUNKS = 2
SMALL = 10 * 1024 * 1024
SHIFTS = (2, 1, 3, 0)
ORDER = (0, 1, 3, 2)
Z_ORDER = (2, 1, 3)
FLOPS_PER_US = 1_150_000_000
BESIDE_X0 = 3
BESIDE_FIRST, BESIDE_KV, BESIDE_Q, BESIDE_MIX = 5, 2, 4, 4
DIAG = False
AXES = ("section", "ctx", "tp")


def send(block, by_tp=0, by_z=0, other_half=False, other_core=False, next_layer=False):
    n_section = lax.axis_size("section")
    n_ctx = lax.axis_size("ctx")
    n_tp = lax.axis_size("tp")
    n_half = n_ctx // 2
    route = []
    for e, c, t in itertools.product(range(n_section), range(n_ctx), range(n_tp)):
        there = (c % n_half + 2 * by_z) % n_half + c // n_half * n_half
        if other_half or next_layer:
            there = (there + n_half) % n_ctx
        if other_core:
            there = there ^ 1
        end = (e + next_layer) % n_section
        route.append(
            ((e * n_ctx + c) * n_tp + t, (end * n_ctx + there) * n_tp + (t + by_tp) % n_tp)
        )
    return lax.ppermute(block, AXES, route)


def in_vmem(kernel, operands, out_shape, name, in_hbm=(), scratch=(), flops=0, beside=0):
    n_bytes = sum(x.size * x.dtype.itemsize for x in (*operands, *in_hbm))
    specs = [pl.BlockSpec(memory_space=pltpu.VMEM)] * len(operands)
    specs += [pl.BlockSpec(memory_space=pl.ANY)] * len(in_hbm)
    return pl.pallas_call(
        kernel,
        in_specs=specs,
        out_specs=[pl.BlockSpec(memory_space=pltpu.VMEM)] * len(out_shape),
        out_shape=[jax.ShapeDtypeStruct(shape, dtype) for shape, dtype in out_shape],
        scratch_shapes=list(scratch),
        compiler_params=pltpu.CompilerParams(vmem_limit_bytes=SMALL),
        cost_estimate=pl.CostEstimate(flops=flops + beside * FLOPS_PER_US, bytes_accessed=n_bytes, transcendentals=0),
        name=name,
    )(*operands, *[pltpu.with_memory_space_constraint(w, pltpu.HBM) for w in in_hbm])


def from_slice(shift, at, width):
    n_tp = lax.axis_size("tp")
    tp = lax.axis_index("tp")
    return pl.multiple_of(lax.rem(tp + (n_tp - shift) % n_tp, n_tp) * width + at, HS)


def scaled_piece(rows_of, gain, start):
    x = jnp.concatenate([r[...] for r in rows_of], axis=0).astype(jnp.float32)
    g = gain[:, pl.ds(start, x.shape[1])]
    return (x * g).astype(jnp.bfloat16), jnp.sum(x * x, axis=-1, keepdims=True)


def rotated(u, cos, sin):
    return u * cos + pltpu.roll(u, HS // 2, 1) * sin


def flat_pieces(pieces):
    return [r for _, _, rows_of in pieces for r in rows_of]


def regroup(refs, pieces):
    out, at = [], 0
    for _, _, rows_of in pieces:
        out.append(refs[at : at + len(rows_of)])
        at += len(rows_of)
    return out, refs[at:]


def rows_of_segments(tokens):
    _, half, width = tokens.shape
    n_half = lax.axis_size("ctx") // 2

    def body(tokens_ref, own, other, sems):
        x_lo = lax.axis_index("ctx") // n_half
        copies = [
            pltpu.make_async_copy(tokens_ref.at[x_lo], own, sems.at[0]),
            pltpu.make_async_copy(tokens_ref.at[1 - x_lo], other, sems.at[1]),
        ]
        for c in copies:
            c.start()
        for c in copies:
            c.wait()

    return in_vmem(
        body,
        [],
        [((half, width), tokens.dtype)] * 2,
        "rows_of_segments",
        in_hbm=[tokens],
        scratch=[pltpu.SemaphoreType.DMA((2,))],
        beside=BESIDE_FIRST,
    )


def stacked(upper, lower):
    rows, width = upper.shape

    def body(a, b, out):
        out[:rows] = a[...]
        out[rows:] = b[...]

    return in_vmem(
        body, [upper, lower], [((2 * rows, width), upper.dtype)], "stacked", beside=BESIDE_X0
    )[0]


def project_kv(pieces, slice_width, gain, wk, wv, carry, rope):
    rows = sum(x.shape[0] for x in pieces[0][2])
    width = pieces[0][2][0].shape[1]
    kv_cols = wk.shape[2]
    n = len(pieces)
    first, last = carry is None, rope is not None

    def body(*refs):
        groups, refs = regroup(refs, pieces)
        gain_ref, wk_ref, wv_ref = refs[:3]
        refs = refs[3:]
        ss = k = v = None
        if not first:
            acc_in, ss_in = refs[:2]
            refs = refs[2:]
            ss, k, v = ss_in[...], acc_in[:, :kv_cols], acc_in[:, kv_cols:]
        for (shift, at, _), rows_of in zip(pieces, groups):
            start = from_slice(shift, at, slice_width)
            x, squares = scaled_piece(rows_of, gain_ref, start)
            here = pl.ds(start, width)
            pk = jnp.dot(x, wk_ref[0, here, :], preferred_element_type=jnp.float32)
            pv = jnp.dot(x, wv_ref[0, here, :], preferred_element_type=jnp.float32)
            ss = squares if ss is None else ss + squares
            k = pk if k is None else k + pk
            v = pv if v is None else v + pv
        if last:
            cos, sin, out, r_out = refs
            r = lax.rsqrt(ss / 4096.0 + EPS)
            r_out[...] = r
            for h in range(kv_cols // HS):
                at = slice(h * HS, (h + 1) * HS)
                out[:, at] = rotated(k[:, at] * r, cos[...], sin[...]).astype(jnp.bfloat16)
            out[:, kv_cols:] = (v * r).astype(jnp.bfloat16)
        else:
            acc, ss_out = refs
            acc[:, :kv_cols] = k
            acc[:, kv_cols:] = v
            ss_out[...] = ss

    operands = flat_pieces(pieces) + [gain, wk, wv]
    operands += [] if first else list(carry)
    operands += list(rope) if last else []
    kind = jnp.bfloat16 if last else jnp.float32
    return in_vmem(
        body,
        operands,
        [((rows, 2 * kv_cols), kind), ((rows, 1), jnp.float32)],
        "project_kv",
        flops=4 * rows * n * width * kv_cols,
        beside=BESIDE_KV,
    )


def project_q(pieces, slice_width, gain, wq, r, rope):
    rows = sum(x.shape[0] for x in pieces[0][2])
    width = pieces[0][2][0].shape[1]
    cols = wq.shape[2]

    def body(*refs):
        groups, refs = regroup(refs, pieces)
        gain_ref, w_ref, r_ref, cos, sin, out = refs
        acc = None
        for (shift, at, _), rows_of in zip(pieces, groups):
            start = from_slice(shift, at, slice_width)
            x, _ = scaled_piece(rows_of, gain_ref, start)
            part = jnp.dot(
                x, w_ref[0, pl.ds(start, width), :], preferred_element_type=jnp.float32
            )
            acc = part if acc is None else acc + part
        r = r_ref[...] * (math.log2(math.e) / math.sqrt(HS))
        for h in range(cols // HS):
            at = slice(h * HS, (h + 1) * HS)
            out[:, at] = rotated(acc[:, at] * r, cos[...], sin[...]).astype(jnp.bfloat16)

    return in_vmem(
        body,
        flat_pieces(pieces) + [gain, wq, r, *rope],
        [((rows, cols), jnp.bfloat16)],
        "project_q",
        flops=2 * rows * wq.size,
        beside=BESIDE_Q,
    )[0]


def attend_and_project(q, qpos, kpos, blocks, w_out, width, layer, parts):
    rows, q_cols = q.shape
    kv_heads = blocks[0].shape[1] // (2 * HS)
    group = q_cols // HS // kv_heads
    n_blocks = len(blocks)
    half = rows // 2
    keys = half * n_blocks
    n_half = lax.axis_size("ctx") // 2
    slice_width = w_out.shape[2] // lax.axis_size("tp")

    def body(q, qpos, kpos, *refs):
        block_refs, refs = refs[:n_blocks], refs[n_blocks:]
        w_ref, *outs, attended = refs
        x_lo = lax.axis_index("ctx") // n_half
        early = x_lo if layer == 0 else 1 - x_lo
        low = pl.ds(pl.multiple_of(early * half, half), half)
        high = pl.ds(pl.multiple_of((1 - early) * half, half), half)
        bias = jnp.where(kpos[...] <= qpos[...], 0.0, -1e30)
        ones = jnp.ones((keys, HS), jnp.bfloat16)

        def keys_of(rows_of, g):
            return jnp.concatenate(
                [b[rows_of, g * HS : (g + 1) * HS] for b in block_refs], axis=0
            )

        def values_of(rows_of, g):
            return jnp.concatenate([keys_of(rows_of, kv_heads + g), ones], axis=1)

        def score(qs, k):
            return lax.dot_general(
                qs, k, (((1,), (1,)), ((), ())), preferred_element_type=jnp.float32
            ).reshape(group, half, keys)

        def weigh(scores, best, v):
            weights = jnp.exp2(scores - best).astype(jnp.bfloat16)
            return jnp.dot(
                weights.reshape(group * half, keys), v, preferred_element_type=jnp.float32
            )

        for g in range(kv_heads):
            heads = [g * group + j for j in range(group)]
            k_low, k_high = keys_of(low, g), keys_of(high, g)
            v_low, v_high = values_of(low, g), values_of(high, g)
            q_low, q_high = (
                jnp.concatenate([q[r, h * HS : (h + 1) * HS] for h in heads], axis=0)
                for r in (low, high)
            )
            same = score(q_low, k_low) + bias[None]
            best = jnp.max(same, axis=-1, keepdims=True)
            acc_low = weigh(same, best, v_low)
            before = score(q_high, k_low)
            same = score(q_high, k_high) + bias[None]
            best = jnp.maximum(
                jnp.max(before, axis=-1, keepdims=True), jnp.max(same, axis=-1, keepdims=True)
            )
            acc_high = weigh(before, best, v_low) + weigh(same, best, v_high)
            for r, acc in ((low, acc_low), (high, acc_high)):
                normal = (acc[:, :HS] / acc[:, HS:]).astype(jnp.bfloat16)
                for j, h in enumerate(heads):
                    attended[r, h * HS : (h + 1) * HS] = normal[j * half : (j + 1) * half]
        project_parts(attended, w_ref, slice_width, width, parts, outs)

    got = in_vmem(
        body,
        [q, qpos, kpos, *blocks, w_out],
        [((n, width), jnp.bfloat16) for *_, n in parts] + [((rows, q_cols), jnp.bfloat16)],
        "attend_and_project",
        flops=6 * rows * q_cols * keys + 2 * rows * w_out.size,
        beside=BESIDE_MIX,
    )
    return got[:-1], got[-1]


def project_parts(attended, w_ref, slice_width, width, parts, outs):
    done = {}
    for (at, shift, row, n), out in zip(parts, outs):
        if (at, shift) not in done:
            there = pl.ds(from_slice(-shift, at, slice_width), width)
            done[at, shift] = jnp.dot(
                attended[...], w_ref[0, :, there], preferred_element_type=jnp.float32
            ).astype(jnp.bfloat16)
        out[...] = done[at, shift][row : row + n]


def project_out(attended, w_out, width, parts):
    slice_width = w_out.shape[2] // lax.axis_size("tp")

    def body(a, w, *outs):
        project_parts(a, w, slice_width, width, parts, outs)

    return in_vmem(
        body,
        [attended, w_out],
        [((n, width), jnp.bfloat16) for *_, n in parts],
        "project_out",
        flops=2 * sum(n for *_, n in parts) * attended.shape[1] * width,
    )


def total_of(parts):
    total = parts[0][...].astype(jnp.float32)
    for p in parts[1:]:
        total = total + p[...].astype(jnp.float32)
    return total


def add_parts(x, at, parts):
    rows, width = parts[0].shape

    def body(x_ref, *refs):
        *refs, out = refs
        x = x_ref[:, at : at + width].astype(jnp.float32)
        out[...] = (x + total_of(refs)).astype(jnp.bfloat16)

    return in_vmem(body, [x, *parts], [((rows, width), jnp.bfloat16)], "add_parts")[0]


def last_cross(kept, x, parts):
    n = len(parts)

    def body(kept_ref, x_ref, *refs):
        section = lax.axis_index("section")
        total = x_ref[...].astype(jnp.float32) + total_of(refs[:n])
        refs[n][...] = jnp.where(section == 0, kept_ref[...], total.astype(jnp.bfloat16))

    return in_vmem(body, [kept, x, *parts], [(x.shape, jnp.bfloat16)], "last_cross")[0]


def finish(kept, x, parts, cross):
    half, width = x.shape
    n = len(parts)
    n_half = lax.axis_size("ctx") // 2

    def body(kept_ref, x_ref, *refs):
        section = lax.axis_index("section")
        x_lo = lax.axis_index("ctx") // n_half
        total = x_ref[...].astype(jnp.float32) + total_of(refs[:n])
        own = jnp.where(section == 0, kept_ref[...], total.astype(jnp.bfloat16))
        cross_ref, out = refs[n:]
        own_first = x_lo == section
        out[0, 0] = jnp.where(own_first, own, cross_ref[...])
        out[0, 1] = jnp.where(own_first, cross_ref[...], own)

    return in_vmem(
        body, [kept, x, *parts, cross], [((1, 2, half, width), jnp.bfloat16)], "finish"
    )[0]


def per_device(tokens, norm_gain, wq, wk, wv, w_out):
    n_ctx = lax.axis_size("ctx")
    n_tp = lax.axis_size("tp")
    n_z = n_ctx // 4
    ctx = lax.axis_index("ctx")
    x_lo = ctx // (n_ctx // 2)
    z = (ctx // 2) % n_z
    core = ctx % 2
    half = tokens.shape[1]
    width = tokens.shape[2]
    chunk = width // CHUNKS

    local = lax.iota(jnp.int32, half)

    def positions(z_of, core_of):
        base = (z_of * 2 + core_of) * half + local
        mine = x_lo * (n_ctx // 2) * half + base
        theirs = (1 - x_lo) * (n_ctx // 2) * half + base
        return jnp.concatenate([mine, theirs])

    z_of = [(z - s) % n_z for s in (0, *Z_ORDER)]
    positions_of = positions(z, core)
    qpos = ((z * 2 + core) * half + local)[:, None]
    kpos = jnp.concatenate(
        [(zs * 2 + c) * half + local for c in (core, 1 - core) for zs in z_of]
    )[None, :]

    def tables(qpos):
        pairs = lax.iota(jnp.int32, HS // 2).astype(jnp.float32)
        freqs = jnp.power(jnp.float32(500000.0), -2.0 * pairs / HS)
        angle = qpos.astype(jnp.float32)[:, None] * freqs[None, :]
        cosine = jnp.cos(angle)
        sine = jnp.sin(angle)
        return (
            jnp.concatenate([cosine, cosine], axis=1),
            jnp.concatenate([-sine, sine], axis=1),
        )

    def swapped(rows):
        return jnp.concatenate([rows[half : 2 * half], rows[:half]], axis=0)


    def mix(kv, make_q, w_out, width, layer, parts):
        theirs = [send(kv, other_core=True)]
        sent = {s: send(kv, by_z=s) for s in (3, 1, 2)}
        q, early = lax.optimization_barrier((make_q(), sent[Z_ORDER[-1]]))
        sent[Z_ORDER[-1]] = early
        mine = [sent[s] for s in Z_ORDER]
        theirs += [send(block, other_core=True) for block in mine]
        blocks = [kv, *mine, *theirs]
        return attend_and_project(q, qpos, kpos, blocks, w_out, width, layer, parts)

    own, other = rows_of_segments(tokens)
    own_from = {s: send(own, by_tp=s) for s in (3, 1, 2)}
    other = send(other, other_half=True)
    positions_of, gain, qpos, kpos, other = lax.optimization_barrier(
        (positions_of, norm_gain, qpos, kpos, other)
    )
    gain = gain.astype(jnp.float32)
    rope = tables(positions_of)
    other_from = {s: send(other, by_tp=s) for s in (3, 1, 2)}
    own_from[0], other_from[0] = own, other
    x0 = stacked(own, other)
    pieces = [(s, 0, [x0] if s == 0 else [own_from[s], other_from[s]]) for s in (0, 2, 1, 3)]
    carry = project_kv(pieces[:2], width, gain, wk, wv, None, None)
    kv, r = project_kv(pieces[2:], width, gain, wk, wv, carry, rope)
    chunked = [[(c * chunk, s, 0, 2 * half) for s in SHIFTS] for c in range(CHUNKS)]
    got, attended = mix(
        kv,
        lambda: project_q(pieces, width, gain, wq, r, rope),
        w_out,
        chunk,
        0,
        chunked[0],
    )
    got += project_out(attended, w_out, chunk, sum(chunked[1:], []))
    sums = []
    for c in range(CHUNKS):
        parts = []
        for s, block in zip(SHIFTS, got[c * n_tp : (c + 1) * n_tp]):
            parts.append(send(block, by_tp=s) if s else block)
        sums.append(add_parts(x0, c * chunk, parts))

    rope = tuple(swapped(t) for t in rope)
    carry = None
    every = []
    came = []
    for c in range(CHUNKS):
        last = c == CHUNKS - 1
        came.append(send(sums[c], next_layer=True))
        x_from = {0: came[c]}
        if DIAG:
            x_from[2] = send(sums[c], next_layer=True, by_tp=2)
        for s in (1, 3) if DIAG else (3, 1, 2):
            x_from[s] = send(came[c], by_tp=s)
        pieces = [(s, c * chunk, [x_from[s]]) for s in ORDER]
        every += pieces
        carry = project_kv(pieces, width, gain, wk, wv, carry, rope if last else None)
    kv, r = carry
    kept = jnp.concatenate(sums, axis=1)
    x1 = jnp.concatenate(came, axis=1)
    got, attended = mix(
        kv,
        lambda: project_q(every, width, gain, wq, r, rope),
        w_out,
        width,
        1,
        [(0, s, row, half) for row in (0, half) for s in SHIFTS],
    )
    rest = got[n_tp:]
    parts = [send(block, by_tp=s) if s else block for s, block in zip(SHIFTS, got)]
    cross = send(last_cross(kept[half:], x1[:half], parts), other_half=True)
    parts = [send(block, by_tp=s) if s else block for s, block in zip(SHIFTS, rest)]
    return finish(kept[:half], x1[half:], parts, cross)


def solution(mesh):
    return jax.shard_map(
        per_device,
        mesh=mesh,
        in_specs=(
            P(None, "ctx", "tp"),
            P("section", None),
            P("section", None, "tp"),
            P("section", None, "tp"),
            P("section", None, "tp"),
            P("section", "tp", None),
        ),
        out_specs=P("section", None, "ctx", "tp"),
        check_vma=False,
    )
```

```python
import itertools
import math
import jax
import jax.numpy as jnp
from jax import lax
from jax.experimental import pallas as pl
from jax.experimental.pallas import tpu as pltpu
from jax.sharding import PartitionSpec as P

HS = 128
EPS = 1e-05
CHUNKS = 2
SMALL = 10 * 1024 * 1024
SHIFTS = (2, 1, 3, 0)
ORDER = (0, 1, 3, 2)
Z_ORDER = (3, 2, 1)
FLOPS_PER_US = 1_150_000_000
BESIDE_GAIN = 3
BESIDE_FIRST, BESIDE_KV, BESIDE_Q, BESIDE_MIX = 5, 2, 4, 4
DIAG = False
AXES = ("section", "ctx", "tp")


def send(block, by_tp=0, by_z=0, other_half=False, other_core=False, next_layer=False):
    n_section = lax.axis_size("section")
    n_ctx = lax.axis_size("ctx")
    n_tp = lax.axis_size("tp")
    n_half = n_ctx // 2
    route = []
    for e, c, t in itertools.product(range(n_section), range(n_ctx), range(n_tp)):
        there = (c % n_half + 2 * by_z) % n_half + c // n_half * n_half
        if other_half or next_layer:
            there = (there + n_half) % n_ctx
        if other_core:
            there = there ^ 1
        end = (e + next_layer) % n_section
        route.append(
            ((e * n_ctx + c) * n_tp + t, (end * n_ctx + there) * n_tp + (t + by_tp) % n_tp)
        )
    return lax.ppermute(block, AXES, route)


def in_vmem(kernel, operands, out_shape, name, in_hbm=(), scratch=(), flops=0, beside=0):
    n_bytes = sum(x.size * x.dtype.itemsize for x in (*operands, *in_hbm))
    specs = [pl.BlockSpec(memory_space=pltpu.VMEM)] * len(operands)
    specs += [pl.BlockSpec(memory_space=pl.ANY)] * len(in_hbm)
    return pl.pallas_call(
        kernel,
        in_specs=specs,
        out_specs=[pl.BlockSpec(memory_space=pltpu.VMEM)] * len(out_shape),
        out_shape=[jax.ShapeDtypeStruct(shape, dtype) for shape, dtype in out_shape],
        scratch_shapes=list(scratch),
        compiler_params=pltpu.CompilerParams(vmem_limit_bytes=SMALL),
        cost_estimate=pl.CostEstimate(flops=flops + beside * FLOPS_PER_US, bytes_accessed=n_bytes, transcendentals=0),
        name=name,
    )(*operands, *[pltpu.with_memory_space_constraint(w, pltpu.HBM) for w in in_hbm])


def from_slice(shift, at, width):
    n_tp = lax.axis_size("tp")
    tp = lax.axis_index("tp")
    return pl.multiple_of(lax.rem(tp + (n_tp - shift) % n_tp, n_tp) * width + at, HS)


def scaled_piece(rows_of, gain, start):
    x = jnp.concatenate([r[...] for r in rows_of], axis=0).astype(jnp.float32)
    g = gain[:, pl.ds(start, x.shape[1])]
    return (x * g).astype(jnp.bfloat16), jnp.sum(x * x, axis=-1, keepdims=True)


def rotated(u, cos, sin):
    return u * cos + pltpu.roll(u, HS // 2, 1) * sin


def flat_pieces(pieces):
    most = max(len(rows_of) for _, _, rows_of in pieces)
    return [rows_of[n] for n in range(most) for _, _, rows_of in pieces if n < len(rows_of)]


def regroup(refs, pieces):
    out = [[] for _ in pieces]
    at = 0
    for n in range(max(len(rows_of) for _, _, rows_of in pieces)):
        for j, (_, _, rows_of) in enumerate(pieces):
            if n < len(rows_of):
                out[j].append(refs[at])
                at += 1
    return out, refs[at:]


def rows_of_segments(tokens):
    _, half, width = tokens.shape
    n_half = lax.axis_size("ctx") // 2

    def body(tokens_ref, own, other, sems):
        x_lo = lax.axis_index("ctx") // n_half
        copies = [
            pltpu.make_async_copy(tokens_ref.at[x_lo], own, sems.at[0]),
            pltpu.make_async_copy(tokens_ref.at[1 - x_lo], other, sems.at[1]),
        ]
        for c in copies:
            c.start()
        for c in copies:
            c.wait()

    return in_vmem(
        body,
        [],
        [((half, width), tokens.dtype)] * 2,
        "rows_of_segments",
        in_hbm=[tokens],
        scratch=[pltpu.SemaphoreType.DMA((2,))],
        beside=BESIDE_FIRST,
    )


def stacked(upper, lower):
    rows, width = upper.shape

    def body(a, b, out):
        out[:rows] = a[...]
        out[rows:] = b[...]

    return in_vmem(
        body, [upper, lower], [((2 * rows, width), upper.dtype)], "stacked"
    )[0]


def widened(gain):
    def body(g, out):
        out[...] = g[...].astype(jnp.float32)

    return in_vmem(
        body, [gain], [(gain.shape, jnp.float32)], "widened", beside=BESIDE_GAIN
    )[0]


def project_kv(pieces, slice_width, gain, wk, wv, carry, rope):
    rows = sum(x.shape[0] for x in pieces[0][2])
    width = pieces[0][2][0].shape[1]
    kv_cols = wk.shape[2]
    n = len(pieces)
    first, last = carry is None, rope is not None

    def body(*refs):
        groups, refs = regroup(refs, pieces)
        gain_ref, wk_ref, wv_ref = refs[:3]
        refs = refs[3:]
        ss = k = v = None
        if not first:
            acc_in, ss_in = refs[:2]
            refs = refs[2:]
            ss, k, v = ss_in[...], acc_in[:, :kv_cols], acc_in[:, kv_cols:]
        for (shift, at, _), rows_of in zip(pieces, groups):
            start = from_slice(shift, at, slice_width)
            x, squares = scaled_piece(rows_of, gain_ref, start)
            here = pl.ds(start, width)
            pk = jnp.dot(x, wk_ref[0, here, :], preferred_element_type=jnp.float32)
            pv = jnp.dot(x, wv_ref[0, here, :], preferred_element_type=jnp.float32)
            ss = squares if ss is None else ss + squares
            k = pk if k is None else k + pk
            v = pv if v is None else v + pv
        if last:
            cos, sin, out, r_out = refs
            r = lax.rsqrt(ss / 4096.0 + EPS)
            r_out[...] = r
            for h in range(kv_cols // HS):
                at = slice(h * HS, (h + 1) * HS)
                out[:, at] = rotated(k[:, at] * r, cos[...], sin[...]).astype(jnp.bfloat16)
            out[:, kv_cols:] = (v * r).astype(jnp.bfloat16)
        else:
            acc, ss_out = refs
            acc[:, :kv_cols] = k
            acc[:, kv_cols:] = v
            ss_out[...] = ss

    operands = flat_pieces(pieces) + [gain, wk, wv]
    operands += [] if first else list(carry)
    operands += list(rope) if last else []
    kind = jnp.bfloat16 if last else jnp.float32
    return in_vmem(
        body,
        operands,
        [((rows, 2 * kv_cols), kind), ((rows, 1), jnp.float32)],
        "project_kv",
        flops=4 * rows * n * width * kv_cols,
        beside=BESIDE_KV,
    )


def project_q(pieces, slice_width, gain, wq, r, rope):
    rows = sum(x.shape[0] for x in pieces[0][2])
    width = pieces[0][2][0].shape[1]
    cols = wq.shape[2]

    def body(*refs):
        groups, refs = regroup(refs, pieces)
        gain_ref, w_ref, r_ref, cos, sin, out = refs
        acc = None
        for (shift, at, _), rows_of in zip(pieces, groups):
            start = from_slice(shift, at, slice_width)
            x, _ = scaled_piece(rows_of, gain_ref, start)
            part = jnp.dot(
                x, w_ref[0, pl.ds(start, width), :], preferred_element_type=jnp.float32
            )
            acc = part if acc is None else acc + part
        r = r_ref[...] * (math.log2(math.e) / math.sqrt(HS))
        for h in range(cols // HS):
            at = slice(h * HS, (h + 1) * HS)
            out[:, at] = rotated(acc[:, at] * r, cos[...], sin[...]).astype(jnp.bfloat16)

    return in_vmem(
        body,
        flat_pieces(pieces) + [gain, wq, r, *rope],
        [((rows, cols), jnp.bfloat16)],
        "project_q",
        flops=2 * rows * wq.size,
        beside=BESIDE_Q,
    )[0]


def attend_and_project(q, qpos, kpos, blocks, w_out, width, layer, parts):
    rows, q_cols = q.shape
    kv_heads = blocks[0].shape[1] // (2 * HS)
    group = q_cols // HS // kv_heads
    n_blocks = len(blocks)
    half = rows // 2
    keys = half * n_blocks
    n_half = lax.axis_size("ctx") // 2
    slice_width = w_out.shape[2] // lax.axis_size("tp")

    def body(q, qpos, kpos, *refs):
        block_refs, refs = refs[:n_blocks], refs[n_blocks:]
        w_ref, *outs, attended = refs
        x_lo = lax.axis_index("ctx") // n_half
        early = x_lo if layer == 0 else 1 - x_lo
        low = pl.ds(pl.multiple_of(early * half, half), half)
        high = pl.ds(pl.multiple_of((1 - early) * half, half), half)
        bias = jnp.where(kpos[...] <= qpos[...], 0.0, -1e30)
        ones = jnp.ones((keys, HS), jnp.bfloat16)

        def keys_of(rows_of, g):
            return jnp.concatenate(
                [b[rows_of, g * HS : (g + 1) * HS] for b in block_refs], axis=0
            )

        def values_of(rows_of, g):
            return jnp.concatenate([keys_of(rows_of, kv_heads + g), ones], axis=1)

        def score(qs, k):
            return lax.dot_general(
                qs, k, (((1,), (1,)), ((), ())), preferred_element_type=jnp.float32
            ).reshape(group, half, keys)

        def weigh(scores, best, v):
            weights = jnp.exp2(scores - best).astype(jnp.bfloat16)
            return jnp.dot(
                weights.reshape(group * half, keys), v, preferred_element_type=jnp.float32
            )

        for g in range(kv_heads):
            heads = [g * group + j for j in range(group)]
            k_low, k_high = keys_of(low, g), keys_of(high, g)
            v_low, v_high = values_of(low, g), values_of(high, g)
            q_low, q_high = (
                jnp.concatenate([q[r, h * HS : (h + 1) * HS] for h in heads], axis=0)
                for r in (low, high)
            )
            same = score(q_low, k_low) + bias[None]
            best = jnp.max(same, axis=-1, keepdims=True)
            acc_low = weigh(same, best, v_low)
            before = score(q_high, k_low)
            same = score(q_high, k_high) + bias[None]
            best = jnp.maximum(
                jnp.max(before, axis=-1, keepdims=True), jnp.max(same, axis=-1, keepdims=True)
            )
            acc_high = weigh(before, best, v_low) + weigh(same, best, v_high)
            for r, acc in ((low, acc_low), (high, acc_high)):
                normal = (acc[:, :HS] / acc[:, HS:]).astype(jnp.bfloat16)
                for j, h in enumerate(heads):
                    attended[r, h * HS : (h + 1) * HS] = normal[j * half : (j + 1) * half]
        project_parts(attended, w_ref, slice_width, width, parts, outs)

    got = in_vmem(
        body,
        [q, qpos, kpos, *blocks, w_out],
        [((n, width), jnp.bfloat16) for *_, n in parts] + [((rows, q_cols), jnp.bfloat16)],
        "attend_and_project",
        flops=6 * rows * q_cols * keys + 2 * rows * w_out.size,
        beside=BESIDE_MIX,
    )
    return got[:-1], got[-1]


def project_parts(attended, w_ref, slice_width, width, parts, outs):
    done = {}
    for (at, shift, row, n), out in zip(parts, outs):
        if (at, shift) not in done:
            there = pl.ds(from_slice(-shift, at, slice_width), width)
            done[at, shift] = jnp.dot(
                attended[...], w_ref[0, :, there], preferred_element_type=jnp.float32
            ).astype(jnp.bfloat16)
        out[...] = done[at, shift][row : row + n]


def project_out(attended, w_out, width, parts):
    slice_width = w_out.shape[2] // lax.axis_size("tp")

    def body(a, w, *outs):
        project_parts(a, w, slice_width, width, parts, outs)

    return in_vmem(
        body,
        [attended, w_out],
        [((n, width), jnp.bfloat16) for *_, n in parts],
        "project_out",
        flops=2 * sum(n for *_, n in parts) * attended.shape[1] * width,
    )


def total_of(parts):
    total = parts[0][...].astype(jnp.float32)
    for p in parts[1:]:
        total = total + p[...].astype(jnp.float32)
    return total


def add_parts(x, at, parts):
    rows, width = parts[0].shape

    def body(*refs):
        *refs, x_ref, out = refs
        x = x_ref[:, at : at + width].astype(jnp.float32)
        out[...] = (x + total_of(refs)).astype(jnp.bfloat16)

    return in_vmem(body, [*parts, x], [((rows, width), jnp.bfloat16)], "add_parts")[0]


def last_cross(kept, x, parts):
    def body(*refs):
        *refs, kept_ref, x_ref, out = refs
        section = lax.axis_index("section")
        total = x_ref[...].astype(jnp.float32) + total_of(refs)
        out[...] = jnp.where(section == 0, kept_ref[...], total.astype(jnp.bfloat16))

    return in_vmem(body, [*parts, kept, x], [(x.shape, jnp.bfloat16)], "last_cross")[0]


def finish(kept, x, parts, cross):
    half, width = x.shape
    n_half = lax.axis_size("ctx") // 2

    def body(*refs):
        *refs, cross_ref, kept_ref, x_ref, out = refs
        section = lax.axis_index("section")
        x_lo = lax.axis_index("ctx") // n_half
        total = x_ref[...].astype(jnp.float32) + total_of(refs)
        own = jnp.where(section == 0, kept_ref[...], total.astype(jnp.bfloat16))
        own_first = x_lo == section
        out[0, 0] = jnp.where(own_first, own, cross_ref[...])
        out[0, 1] = jnp.where(own_first, cross_ref[...], own)

    return in_vmem(
        body, [*parts, cross, kept, x], [((1, 2, half, width), jnp.bfloat16)], "finish"
    )[0]


def per_device(tokens, norm_gain, wq, wk, wv, w_out):
    n_ctx = lax.axis_size("ctx")
    n_tp = lax.axis_size("tp")
    n_z = n_ctx // 4
    ctx = lax.axis_index("ctx")
    x_lo = ctx // (n_ctx // 2)
    z = (ctx // 2) % n_z
    core = ctx % 2
    half = tokens.shape[1]
    width = tokens.shape[2]
    chunk = width // CHUNKS

    local = lax.iota(jnp.int32, half)

    def positions(z_of, core_of):
        base = (z_of * 2 + core_of) * half + local
        mine = x_lo * (n_ctx // 2) * half + base
        theirs = (1 - x_lo) * (n_ctx // 2) * half + base
        return jnp.concatenate([mine, theirs])

    z_of = [(z - s) % n_z for s in (0, *Z_ORDER)]
    positions_of = positions(z, core)
    qpos = ((z * 2 + core) * half + local)[:, None]
    kpos = jnp.concatenate(
        [(zs * 2 + c) * half + local for c in (core, 1 - core) for zs in z_of]
    )[None, :]

    def tables(qpos):
        pairs = lax.iota(jnp.int32, HS // 2).astype(jnp.float32)
        freqs = jnp.power(jnp.float32(500000.0), -2.0 * pairs / HS)
        angle = qpos.astype(jnp.float32)[:, None] * freqs[None, :]
        cosine = jnp.cos(angle)
        sine = jnp.sin(angle)
        return (
            jnp.concatenate([cosine, cosine], axis=1),
            jnp.concatenate([-sine, sine], axis=1),
        )

    def swapped(rows):
        return jnp.concatenate([rows[half : 2 * half], rows[:half]], axis=0)


    def mix(kv, make_q, w_out, width, layer, parts):
        theirs = send(kv, other_core=True)
        sent = {s: send(kv, by_z=s) for s in Z_ORDER}
        first = Z_ORDER[0]
        q, theirs, sent[first] = lax.optimization_barrier((make_q(), theirs, sent[first]))
        mine = [sent[s] for s in Z_ORDER]
        theirs = [theirs] + [send(block, other_core=True) for block in mine]
        blocks = [kv, *mine, *theirs]
        return attend_and_project(q, qpos, kpos, blocks, w_out, width, layer, parts)

    own, other = rows_of_segments(tokens)
    own_from = {s: send(own, by_tp=s) for s in (3, 1, 2)}
    other = send(other, other_half=True)
    positions_of, gain, qpos, kpos, other = lax.optimization_barrier(
        (positions_of, norm_gain, qpos, kpos, other)
    )
    gain = widened(gain)
    rope = tables(positions_of)
    other_from = {s: send(other, by_tp=s) for s in (3, 1, 2)}
    own_from[0], other_from[0] = own, other
    pieces = [(s, 0, [own_from[s], other_from[s]]) for s in (1, 3, 0, 2)]
    carry = project_kv(pieces[:2], width, gain, wk, wv, None, None)
    kv, r = project_kv(pieces[2:], width, gain, wk, wv, carry, rope)
    chunked = [[(c * chunk, s, 0, 2 * half) for s in SHIFTS] for c in range(CHUNKS)]
    got, attended = mix(
        kv,
        lambda: project_q(pieces, width, gain, wq, r, rope),
        w_out,
        chunk,
        0,
        chunked[0],
    )
    got += project_out(attended, w_out, chunk, sum(chunked[1:], []))
    x0 = stacked(own, other)
    sums = []
    for c in range(CHUNKS):
        parts = []
        for s, block in zip(SHIFTS, got[c * n_tp : (c + 1) * n_tp]):
            parts.append(send(block, by_tp=s) if s else block)
        sums.append(add_parts(x0, c * chunk, parts))

    rope = tuple(swapped(t) for t in rope)
    carry = None
    every = []
    came = []
    for c in range(CHUNKS):
        last = c == CHUNKS - 1
        came.append(send(sums[c], next_layer=True))
        x_from = {0: came[c]}
        if DIAG:
            x_from[2] = send(sums[c], next_layer=True, by_tp=2)
        for s in (1, 3) if DIAG else (3, 1, 2):
            x_from[s] = send(came[c], by_tp=s)
        pieces = [(s, c * chunk, [x_from[s]]) for s in ORDER]
        every += pieces
        carry = project_kv(pieces, width, gain, wk, wv, carry, rope if last else None)
    kv, r = carry
    kept = jnp.concatenate(sums, axis=1)
    x1 = jnp.concatenate(came, axis=1)
    got, attended = mix(
        kv,
        lambda: project_q(every, width, gain, wq, r, rope),
        w_out,
        width,
        1,
        [(0, s, row, half) for row in (0, half) for s in SHIFTS],
    )
    rest = got[n_tp:]
    parts = [send(block, by_tp=s) if s else block for s, block in zip(SHIFTS, got)]
    cross = send(last_cross(kept[half:], x1[:half], parts), other_half=True)
    parts = [send(block, by_tp=s) if s else block for s, block in zip(SHIFTS, rest)]
    return finish(kept[:half], x1[half:], parts, cross)


def solution(mesh):
    return jax.shard_map(
        per_device,
        mesh=mesh,
        in_specs=(
            P(None, "ctx", "tp"),
            P("section", None),
            P("section", None, "tp"),
            P("section", None, "tp"),
            P("section", None, "tp"),
            P("section", "tp", None),
        ),
        out_specs=P("section", None, "ctx", "tp"),
        check_vma=False,
    )
```

```python
import itertools
import math
import jax
import jax.numpy as jnp
from jax import lax
from jax.experimental import pallas as pl
from jax.experimental.pallas import tpu as pltpu
from jax.sharding import PartitionSpec as P

HS = 128
EPS = 1e-05
CHUNKS = (512, 512)
SMALL = 10 * 1024 * 1024
SHIFTS = (2, 1, 3, 0)
ORDER = (0, 1, 3, 2)
Z_ORDER = (3, 1, 2)
FLOPS_PER_US = 1_150_000_000
BESIDE_GAIN = 3
BESIDE_FIRST, BESIDE_KV, BESIDE_Q, BESIDE_MIX = 5, 2, 4, 8
DIAG = (0, 1)
AXES = ("section", "ctx", "tp")


def send(block, by_tp=0, by_z=0, other_half=False, other_core=False, next_layer=False):
    n_section = lax.axis_size("section")
    n_ctx = lax.axis_size("ctx")
    n_tp = lax.axis_size("tp")
    n_half = n_ctx // 2
    route = []
    for e, c, t in itertools.product(range(n_section), range(n_ctx), range(n_tp)):
        there = (c % n_half + 2 * by_z) % n_half + c // n_half * n_half
        if other_half or next_layer:
            there = (there + n_half) % n_ctx
        if other_core:
            there = there ^ 1
        end = (e + next_layer) % n_section
        route.append(
            ((e * n_ctx + c) * n_tp + t, (end * n_ctx + there) * n_tp + (t + by_tp) % n_tp)
        )
    return lax.ppermute(block, AXES, route)


def in_vmem(kernel, operands, out_shape, name, in_hbm=(), scratch=(), flops=0, beside=0):
    n_bytes = sum(x.size * x.dtype.itemsize for x in (*operands, *in_hbm))
    specs = [pl.BlockSpec(memory_space=pltpu.VMEM)] * len(operands)
    specs += [pl.BlockSpec(memory_space=pl.ANY)] * len(in_hbm)
    return pl.pallas_call(
        kernel,
        in_specs=specs,
        out_specs=[pl.BlockSpec(memory_space=pltpu.VMEM)] * len(out_shape),
        out_shape=[jax.ShapeDtypeStruct(shape, dtype) for shape, dtype in out_shape],
        scratch_shapes=list(scratch),
        compiler_params=pltpu.CompilerParams(vmem_limit_bytes=SMALL),
        cost_estimate=pl.CostEstimate(flops=flops + beside * FLOPS_PER_US, bytes_accessed=n_bytes, transcendentals=0),
        name=name,
    )(*operands, *[pltpu.with_memory_space_constraint(w, pltpu.HBM) for w in in_hbm])


def from_slice(shift, at, width):
    n_tp = lax.axis_size("tp")
    tp = lax.axis_index("tp")
    return pl.multiple_of(lax.rem(tp + (n_tp - shift) % n_tp, n_tp) * width + at, HS)


def scaled_piece(rows_of, gain, start):
    x = jnp.concatenate([r[...] for r in rows_of], axis=0).astype(jnp.float32)
    g = gain[:, pl.ds(start, x.shape[1])]
    return (x * g).astype(jnp.bfloat16), jnp.sum(x * x, axis=-1, keepdims=True)


def rotated(u, cos, sin):
    return u * cos + pltpu.roll(u, HS // 2, 1) * sin


def flat_pieces(pieces):
    most = max(len(rows_of) for _, _, rows_of in pieces)
    return [rows_of[n] for n in range(most) for _, _, rows_of in pieces if n < len(rows_of)]


def regroup(refs, pieces):
    out = [[] for _ in pieces]
    at = 0
    for n in range(max(len(rows_of) for _, _, rows_of in pieces)):
        for j, (_, _, rows_of) in enumerate(pieces):
            if n < len(rows_of):
                out[j].append(refs[at])
                at += 1
    return out, refs[at:]


def rows_of_segments(tokens):
    _, half, width = tokens.shape
    n_half = lax.axis_size("ctx") // 2

    def body(tokens_ref, own, other, sems):
        x_lo = lax.axis_index("ctx") // n_half
        copies = [
            pltpu.make_async_copy(tokens_ref.at[x_lo], own, sems.at[0]),
            pltpu.make_async_copy(tokens_ref.at[1 - x_lo], other, sems.at[1]),
        ]
        for c in copies:
            c.start()
        for c in copies:
            c.wait()

    return in_vmem(
        body,
        [],
        [((half, width), tokens.dtype)] * 2,
        "rows_of_segments",
        in_hbm=[tokens],
        scratch=[pltpu.SemaphoreType.DMA((2,))],
        beside=BESIDE_FIRST,
    )


def stacked(upper, lower):
    rows, width = upper.shape

    def body(a, b, out):
        out[:rows] = a[...]
        out[rows:] = b[...]

    return in_vmem(
        body, [upper, lower], [((2 * rows, width), upper.dtype)], "stacked"
    )[0]


def widened(gain):
    def body(g, out):
        out[...] = g[...].astype(jnp.float32)

    return in_vmem(
        body, [gain], [(gain.shape, jnp.float32)], "widened", beside=BESIDE_GAIN
    )[0]


def project_kv(pieces, slice_width, gain, wk, wv, carry, rope):
    rows = sum(x.shape[0] for x in pieces[0][2])
    width = pieces[0][2][0].shape[1]
    kv_cols = wk.shape[2]
    n = len(pieces)
    first, last = carry is None, rope is not None

    def body(*refs):
        groups, refs = regroup(refs, pieces)
        gain_ref, wk_ref, wv_ref = refs[:3]
        refs = refs[3:]
        ss = k = v = None
        if not first:
            acc_in, ss_in = refs[:2]
            refs = refs[2:]
            ss, k, v = ss_in[...], acc_in[:, :kv_cols], acc_in[:, kv_cols:]
        for (shift, at, _), rows_of in zip(pieces, groups):
            start = from_slice(shift, at, slice_width)
            x, squares = scaled_piece(rows_of, gain_ref, start)
            here = pl.ds(start, width)
            pk = jnp.dot(x, wk_ref[0, here, :], preferred_element_type=jnp.float32)
            pv = jnp.dot(x, wv_ref[0, here, :], preferred_element_type=jnp.float32)
            ss = squares if ss is None else ss + squares
            k = pk if k is None else k + pk
            v = pv if v is None else v + pv
        if last:
            cos, sin, out, r_out = refs
            r = lax.rsqrt(ss / 4096.0 + EPS)
            r_out[...] = r
            for h in range(kv_cols // HS):
                at = slice(h * HS, (h + 1) * HS)
                out[:, at] = rotated(k[:, at] * r, cos[...], sin[...]).astype(jnp.bfloat16)
            out[:, kv_cols:] = (v * r).astype(jnp.bfloat16)
        else:
            acc, ss_out = refs
            acc[:, :kv_cols] = k
            acc[:, kv_cols:] = v
            ss_out[...] = ss

    operands = flat_pieces(pieces) + [gain, wk, wv]
    operands += [] if first else list(carry)
    operands += list(rope) if last else []
    kind = jnp.bfloat16 if last else jnp.float32
    return in_vmem(
        body,
        operands,
        [((rows, 2 * kv_cols), kind), ((rows, 1), jnp.float32)],
        "project_kv",
        flops=4 * rows * n * width * kv_cols,
        beside=BESIDE_KV,
    )


def project_q(pieces, slice_width, gain, wq, r, rope):
    rows = sum(x.shape[0] for x in pieces[0][2])
    width = pieces[0][2][0].shape[1]
    cols = wq.shape[2]

    def body(*refs):
        groups, refs = regroup(refs, pieces)
        gain_ref, w_ref, r_ref, cos, sin, out = refs
        acc = None
        for (shift, at, _), rows_of in zip(pieces, groups):
            start = from_slice(shift, at, slice_width)
            x, _ = scaled_piece(rows_of, gain_ref, start)
            part = jnp.dot(
                x, w_ref[0, pl.ds(start, width), :], preferred_element_type=jnp.float32
            )
            acc = part if acc is None else acc + part
        r = r_ref[...] * (math.log2(math.e) / math.sqrt(HS))
        for h in range(cols // HS):
            at = slice(h * HS, (h + 1) * HS)
            out[:, at] = rotated(acc[:, at] * r, cos[...], sin[...]).astype(jnp.bfloat16)

    return in_vmem(
        body,
        flat_pieces(pieces) + [gain, wq, r, *rope],
        [((rows, cols), jnp.bfloat16)],
        "project_q",
        flops=2 * rows * wq.size,
        beside=BESIDE_Q,
    )[0]


def attend_and_project(q, qpos, kpos, blocks, w_out, width, layer, parts):
    rows, q_cols = q.shape
    kv_heads = blocks[0].shape[1] // (2 * HS)
    group = q_cols // HS // kv_heads
    n_blocks = len(blocks)
    half = rows // 2
    keys = half * n_blocks
    n_half = lax.axis_size("ctx") // 2
    slice_width = w_out.shape[2] // lax.axis_size("tp")

    def body(q, qpos, kpos, *refs):
        block_refs, refs = refs[:n_blocks], refs[n_blocks:]
        w_ref, *outs, attended = refs
        x_lo = lax.axis_index("ctx") // n_half
        early = x_lo if layer == 0 else 1 - x_lo
        low = pl.ds(pl.multiple_of(early * half, half), half)
        high = pl.ds(pl.multiple_of((1 - early) * half, half), half)
        bias = jnp.where(kpos[...] <= qpos[...], 0.0, -1e30)
        ones = jnp.ones((keys, HS), jnp.bfloat16)

        def keys_of(rows_of, g):
            return jnp.concatenate(
                [b[rows_of, g * HS : (g + 1) * HS] for b in block_refs], axis=0
            )

        def values_of(rows_of, g):
            return jnp.concatenate([keys_of(rows_of, kv_heads + g), ones], axis=1)

        def score(qs, k):
            return lax.dot_general(
                qs, k, (((1,), (1,)), ((), ())), preferred_element_type=jnp.float32
            ).reshape(group, half, keys)

        def weigh(scores, best, v):
            weights = jnp.exp2(scores - best).astype(jnp.bfloat16)
            return jnp.dot(
                weights.reshape(group * half, keys), v, preferred_element_type=jnp.float32
            )

        for g in range(kv_heads):
            heads = [g * group + j for j in range(group)]
            k_low, k_high = keys_of(low, g), keys_of(high, g)
            v_low, v_high = values_of(low, g), values_of(high, g)
            q_low, q_high = (
                jnp.concatenate([q[r, h * HS : (h + 1) * HS] for h in heads], axis=0)
                for r in (low, high)
            )
            same = score(q_low, k_low) + bias[None]
            best = jnp.max(same, axis=-1, keepdims=True)
            acc_low = weigh(same, best, v_low)
            before = score(q_high, k_low)
            same = score(q_high, k_high) + bias[None]
            best = jnp.maximum(
                jnp.max(before, axis=-1, keepdims=True), jnp.max(same, axis=-1, keepdims=True)
            )
            acc_high = weigh(before, best, v_low) + weigh(same, best, v_high)
            for r, acc in ((low, acc_low), (high, acc_high)):
                normal = (acc[:, :HS] / acc[:, HS:]).astype(jnp.bfloat16)
                for j, h in enumerate(heads):
                    attended[r, h * HS : (h + 1) * HS] = normal[j * half : (j + 1) * half]
        project_parts(attended, w_ref, slice_width, width, parts, outs)

    got = in_vmem(
        body,
        [q, qpos, kpos, *blocks, w_out],
        [((n, width), jnp.bfloat16) for *_, n in parts] + [((rows, q_cols), jnp.bfloat16)],
        "attend_and_project",
        flops=6 * rows * q_cols * keys + 2 * rows * w_out.size,
        beside=BESIDE_MIX,
    )
    return got[:-1], got[-1]


def project_parts(attended, w_ref, slice_width, width, parts, outs):
    done = {}
    for (at, shift, row, n), out in zip(parts, outs):
        if (at, shift) not in done:
            there = pl.ds(from_slice(-shift, at, slice_width), width)
            done[at, shift] = jnp.dot(
                attended[...], w_ref[0, :, there], preferred_element_type=jnp.float32
            ).astype(jnp.bfloat16)
        out[...] = done[at, shift][row : row + n]


def project_out(attended, w_out, width, parts):
    slice_width = w_out.shape[2] // lax.axis_size("tp")

    def body(a, w, *outs):
        project_parts(a, w, slice_width, width, parts, outs)

    return in_vmem(
        body,
        [attended, w_out],
        [((n, width), jnp.bfloat16) for *_, n in parts],
        "project_out",
        flops=2 * sum(n for *_, n in parts) * attended.shape[1] * width,
    )


def total_of(parts):
    total = parts[0][...].astype(jnp.float32)
    for p in parts[1:]:
        total = total + p[...].astype(jnp.float32)
    return total


def add_parts(x, at, parts):
    rows, width = parts[0].shape

    def body(*refs):
        *refs, x_ref, out = refs
        x = x_ref[:, at : at + width].astype(jnp.float32)
        out[...] = (x + total_of(refs)).astype(jnp.bfloat16)

    return in_vmem(body, [*parts, x], [((rows, width), jnp.bfloat16)], "add_parts")[0]


def last_cross(kept, x, parts):
    def body(*refs):
        *refs, kept_ref, x_ref, out = refs
        section = lax.axis_index("section")
        total = x_ref[...].astype(jnp.float32) + total_of(refs)
        out[...] = jnp.where(section == 0, kept_ref[...], total.astype(jnp.bfloat16))

    return in_vmem(body, [*parts, kept, x], [(x.shape, jnp.bfloat16)], "last_cross")[0]


def finish(kept, x, parts, cross):
    half, width = x.shape
    n_half = lax.axis_size("ctx") // 2

    def body(*refs):
        *refs, cross_ref, kept_ref, x_ref, out = refs
        section = lax.axis_index("section")
        x_lo = lax.axis_index("ctx") // n_half
        total = x_ref[...].astype(jnp.float32) + total_of(refs)
        own = jnp.where(section == 0, kept_ref[...], total.astype(jnp.bfloat16))
        own_first = x_lo == section
        out[0, 0] = jnp.where(own_first, own, cross_ref[...])
        out[0, 1] = jnp.where(own_first, cross_ref[...], own)

    return in_vmem(
        body, [*parts, cross, kept, x], [((1, 2, half, width), jnp.bfloat16)], "finish"
    )[0]


def per_device(tokens, norm_gain, wq, wk, wv, w_out):
    n_ctx = lax.axis_size("ctx")
    n_tp = lax.axis_size("tp")
    n_z = n_ctx // 4
    ctx = lax.axis_index("ctx")
    x_lo = ctx // (n_ctx // 2)
    z = (ctx // 2) % n_z
    core = ctx % 2
    half = tokens.shape[1]
    width = tokens.shape[2]
    starts = [sum(CHUNKS[:c]) for c in range(len(CHUNKS))]

    local = lax.iota(jnp.int32, half)

    def positions(z_of, core_of):
        base = (z_of * 2 + core_of) * half + local
        mine = x_lo * (n_ctx // 2) * half + base
        theirs = (1 - x_lo) * (n_ctx // 2) * half + base
        return jnp.concatenate([mine, theirs])

    z_of = [(z - s) % n_z for s in (0, *Z_ORDER)]
    positions_of = positions(z, core)
    qpos = ((z * 2 + core) * half + local)[:, None]
    kpos = jnp.concatenate(
        [(zs * 2 + c) * half + local for c in (core, 1 - core) for zs in z_of]
    )[None, :]

    def tables(qpos):
        pairs = lax.iota(jnp.int32, HS // 2).astype(jnp.float32)
        freqs = jnp.power(jnp.float32(500000.0), -2.0 * pairs / HS)
        angle = qpos.astype(jnp.float32)[:, None] * freqs[None, :]
        cosine = jnp.cos(angle)
        sine = jnp.sin(angle)
        return (
            jnp.concatenate([cosine, cosine], axis=1),
            jnp.concatenate([-sine, sine], axis=1),
        )

    def swapped(rows):
        return jnp.concatenate([rows[half : 2 * half], rows[:half]], axis=0)


    def mix(kv, make_q, w_out, width, layer, parts):
        theirs = send(kv, other_core=True)
        sent = {s: send(kv, by_z=s) for s in Z_ORDER}
        first = Z_ORDER[0]
        q, theirs, sent[first] = lax.optimization_barrier((make_q(), theirs, sent[first]))
        mine = [sent[s] for s in Z_ORDER]
        theirs = [theirs] + [send(block, other_core=True) for block in mine]
        blocks = [kv, *mine, *theirs]
        return attend_and_project(q, qpos, kpos, blocks, w_out, width, layer, parts)

    own, other = rows_of_segments(tokens)
    own_from = {s: send(own, by_tp=s) for s in (3, 1, 2)}
    other = send(other, other_half=True)
    positions_of, gain, qpos, kpos, other = lax.optimization_barrier(
        (positions_of, norm_gain, qpos, kpos, other)
    )
    gain = widened(gain)
    rope = tables(positions_of)
    other_from = {s: send(other, by_tp=s) for s in (3, 1, 2)}
    own_from[0], other_from[0] = own, other
    pieces = [(s, 0, [own_from[s], other_from[s]]) for s in (1, 3, 0, 2)]
    carry = project_kv(pieces[:2], width, gain, wk, wv, None, None)
    kv, r = project_kv(pieces[2:], width, gain, wk, wv, carry, rope)
    chunked = [[(at, s, 0, 2 * half) for s in SHIFTS] for at in starts]
    got, attended = mix(
        kv,
        lambda: project_q(pieces, width, gain, wq, r, rope),
        w_out,
        CHUNKS[0],
        0,
        chunked[0],
    )
    for c in range(1, len(CHUNKS)):
        got += project_out(attended, w_out, CHUNKS[c], chunked[c])
    x0 = stacked(own, other)
    sums = []
    for c in range(len(CHUNKS)):
        parts = []
        for s, block in zip(SHIFTS, got[c * n_tp : (c + 1) * n_tp]):
            parts.append(send(block, by_tp=s) if s else block)
        sums.append(add_parts(x0, starts[c], parts))

    rope = tuple(swapped(t) for t in rope)
    carry = None
    every = []
    came = []
    for c in range(len(CHUNKS)):
        last = c == len(CHUNKS) - 1
        came.append(send(sums[c], next_layer=True))
        x_from = {0: came[c]}
        if c in DIAG:
            x_from[2] = send(sums[c], next_layer=True, by_tp=2)
        for s in (1, 3) if c in DIAG else (3, 1, 2):
            x_from[s] = send(came[c], by_tp=s)
        pieces = [(s, starts[c], [x_from[s]]) for s in ORDER]
        every += pieces
        carry = project_kv(pieces, width, gain, wk, wv, carry, rope if last else None)
    kv, r = carry
    kept = jnp.concatenate(sums, axis=1)
    x1 = jnp.concatenate(came, axis=1)
    got, attended = mix(
        kv,
        lambda: project_q(every, width, gain, wq, r, rope),
        w_out,
        width,
        1,
        [(0, s, row, half) for row in (0, half) for s in SHIFTS],
    )
    rest = got[n_tp:]
    parts = [send(block, by_tp=s) if s else block for s, block in zip(SHIFTS, got)]
    cross = send(last_cross(kept[half:], x1[:half], parts), other_half=True)
    parts = [send(block, by_tp=s) if s else block for s, block in zip(SHIFTS, rest)]
    return finish(kept[:half], x1[half:], parts, cross)


def solution(mesh):
    return jax.shard_map(
        per_device,
        mesh=mesh,
        in_specs=(
            P(None, "ctx", "tp"),
            P("section", None),
            P("section", None, "tp"),
            P("section", None, "tp"),
            P("section", None, "tp"),
            P("section", "tp", None),
        ),
        out_specs=P("section", None, "ctx", "tp"),
        check_vma=False,
    )
```

```python
import itertools
import math
import jax
import jax.numpy as jnp
from jax import lax
from jax.experimental import pallas as pl
from jax.experimental.pallas import tpu as pltpu
from jax.sharding import PartitionSpec as P

HS = 128
EPS = 1e-05
CHUNKS = (512, 512)
SMALL = 10 * 1024 * 1024
SHIFTS = (2, 1, 3, 0)
ORDER = (0, 1, 3, 2)
Z_ORDER = (3, 1, 2)
FLOPS_PER_US = 1_150_000_000
BESIDE_GAIN = 3
BESIDE_FIRST, BESIDE_KV, BESIDE_Q, BESIDE_MIX = 5, 2, 4, 8
DIAG = (0, 1)
AXES = ("section", "ctx", "tp")


def send(block, by_tp=0, by_z=0, other_half=False, other_core=False, next_layer=False):
    n_section = lax.axis_size("section")
    n_ctx = lax.axis_size("ctx")
    n_tp = lax.axis_size("tp")
    n_half = n_ctx // 2
    route = []
    for e, c, t in itertools.product(range(n_section), range(n_ctx), range(n_tp)):
        there = (c % n_half + 2 * by_z) % n_half + c // n_half * n_half
        if other_half or next_layer:
            there = (there + n_half) % n_ctx
        if other_core:
            there = there ^ 1
        end = (e + next_layer) % n_section
        route.append(
            ((e * n_ctx + c) * n_tp + t, (end * n_ctx + there) * n_tp + (t + by_tp) % n_tp)
        )
    return lax.ppermute(block, AXES, route)


def in_vmem(kernel, operands, out_shape, name, in_hbm=(), scratch=(), flops=0, beside=0):
    n_bytes = sum(x.size * x.dtype.itemsize for x in (*operands, *in_hbm))
    specs = [pl.BlockSpec(memory_space=pltpu.VMEM)] * len(operands)
    specs += [pl.BlockSpec(memory_space=pl.ANY)] * len(in_hbm)
    return pl.pallas_call(
        kernel,
        in_specs=specs,
        out_specs=[pl.BlockSpec(memory_space=pltpu.VMEM)] * len(out_shape),
        out_shape=[jax.ShapeDtypeStruct(shape, dtype) for shape, dtype in out_shape],
        scratch_shapes=list(scratch),
        compiler_params=pltpu.CompilerParams(vmem_limit_bytes=SMALL),
        cost_estimate=pl.CostEstimate(flops=flops + beside * FLOPS_PER_US, bytes_accessed=n_bytes, transcendentals=0),
        name=name,
    )(*operands, *[pltpu.with_memory_space_constraint(w, pltpu.HBM) for w in in_hbm])


def from_slice(shift, at, width):
    n_tp = lax.axis_size("tp")
    tp = lax.axis_index("tp")
    return pl.multiple_of(lax.rem(tp + (n_tp - shift) % n_tp, n_tp) * width + at, HS)


def scaled_piece(rows_of, gain, start):
    x = jnp.concatenate([r[...] for r in rows_of], axis=0).astype(jnp.float32)
    g = gain[:, pl.ds(start, x.shape[1])]
    return (x * g).astype(jnp.bfloat16), jnp.sum(x * x, axis=-1, keepdims=True)


def rotated(u, cos, sin):
    return u * cos + pltpu.roll(u, HS // 2, 1) * sin


def flat_pieces(pieces):
    most = max(len(rows_of) for _, _, rows_of in pieces)
    return [rows_of[n] for n in range(most) for _, _, rows_of in pieces if n < len(rows_of)]


def regroup(refs, pieces):
    out = [[] for _ in pieces]
    at = 0
    for n in range(max(len(rows_of) for _, _, rows_of in pieces)):
        for j, (_, _, rows_of) in enumerate(pieces):
            if n < len(rows_of):
                out[j].append(refs[at])
                at += 1
    return out, refs[at:]


def rows_of_segments(tokens):
    _, half, width = tokens.shape
    n_half = lax.axis_size("ctx") // 2

    def body(tokens_ref, own, other, sems):
        x_lo = lax.axis_index("ctx") // n_half
        copies = [
            pltpu.make_async_copy(tokens_ref.at[x_lo], own, sems.at[0]),
            pltpu.make_async_copy(tokens_ref.at[1 - x_lo], other, sems.at[1]),
        ]
        for c in copies:
            c.start()
        for c in copies:
            c.wait()

    return in_vmem(
        body,
        [],
        [((half, width), tokens.dtype)] * 2,
        "rows_of_segments",
        in_hbm=[tokens],
        scratch=[pltpu.SemaphoreType.DMA((2,))],
        beside=BESIDE_FIRST,
    )


def stacked(upper, lower):
    rows, width = upper.shape

    def body(a, b, out):
        out[:rows] = a[...]
        out[rows:] = b[...]

    return in_vmem(
        body, [upper, lower], [((2 * rows, width), upper.dtype)], "stacked"
    )[0]


def widened(gain):
    def body(g, out):
        out[...] = g[...].astype(jnp.float32)

    return in_vmem(
        body, [gain], [(gain.shape, jnp.float32)], "widened", beside=BESIDE_GAIN
    )[0]


def project_kv(pieces, slice_width, gain, wk, wv, carry, rope):
    rows = sum(x.shape[0] for x in pieces[0][2])
    width = pieces[0][2][0].shape[1]
    kv_cols = wk.shape[2]
    n = len(pieces)
    first, last = carry is None, rope is not None

    def body(*refs):
        groups, refs = regroup(refs, pieces)
        gain_ref, wk_ref, wv_ref = refs[:3]
        refs = refs[3:]
        ss = k = v = None
        if not first:
            acc_in, ss_in = refs[:2]
            refs = refs[2:]
            ss, k, v = ss_in[...], acc_in[:, :kv_cols], acc_in[:, kv_cols:]
        for (shift, at, _), rows_of in zip(pieces, groups):
            start = from_slice(shift, at, slice_width)
            x, squares = scaled_piece(rows_of, gain_ref, start)
            here = pl.ds(start, width)
            pk = jnp.dot(x, wk_ref[0, here, :], preferred_element_type=jnp.float32)
            pv = jnp.dot(x, wv_ref[0, here, :], preferred_element_type=jnp.float32)
            ss = squares if ss is None else ss + squares
            k = pk if k is None else k + pk
            v = pv if v is None else v + pv
        if last:
            cos, sin, out, r_out = refs
            r = lax.rsqrt(ss / 4096.0 + EPS)
            r_out[...] = r
            for h in range(kv_cols // HS):
                at = slice(h * HS, (h + 1) * HS)
                out[:, at] = rotated(k[:, at] * r, cos[...], sin[...]).astype(jnp.bfloat16)
            out[:, kv_cols:] = (v * r).astype(jnp.bfloat16)
        else:
            acc, ss_out = refs
            acc[:, :kv_cols] = k
            acc[:, kv_cols:] = v
            ss_out[...] = ss

    operands = flat_pieces(pieces) + [gain, wk, wv]
    operands += [] if first else list(carry)
    operands += list(rope) if last else []
    kind = jnp.bfloat16 if last else jnp.float32
    return in_vmem(
        body,
        operands,
        [((rows, 2 * kv_cols), kind), ((rows, 1), jnp.float32)],
        "project_kv",
        flops=4 * rows * n * width * kv_cols,
        beside=BESIDE_KV,
    )


def project_q(pieces, slice_width, gain, wq, r, rope):
    rows = sum(x.shape[0] for x in pieces[0][2])
    width = pieces[0][2][0].shape[1]
    cols = wq.shape[2]

    def body(*refs):
        groups, refs = regroup(refs, pieces)
        gain_ref, w_ref, r_ref, cos, sin, out = refs
        acc = None
        for (shift, at, _), rows_of in zip(pieces, groups):
            start = from_slice(shift, at, slice_width)
            x, _ = scaled_piece(rows_of, gain_ref, start)
            part = jnp.dot(
                x, w_ref[0, pl.ds(start, width), :], preferred_element_type=jnp.float32
            )
            acc = part if acc is None else acc + part
        r = r_ref[...] * (math.log2(math.e) / math.sqrt(HS))
        for h in range(cols // HS):
            at = slice(h * HS, (h + 1) * HS)
            out[:, at] = rotated(acc[:, at] * r, cos[...], sin[...]).astype(jnp.bfloat16)

    return in_vmem(
        body,
        flat_pieces(pieces) + [gain, wq, r, *rope],
        [((rows, cols), jnp.bfloat16)],
        "project_q",
        flops=2 * rows * wq.size,
        beside=BESIDE_Q,
    )[0]


def attend_and_project(q, qpos, kpos, blocks, w_out, width, layer, parts):
    rows, q_cols = q.shape
    kv_heads = blocks[0].shape[1] // (2 * HS)
    group = q_cols // HS // kv_heads
    n_blocks = len(blocks)
    half = rows // 2
    keys = half * n_blocks
    n_half = lax.axis_size("ctx") // 2
    slice_width = w_out.shape[2] // lax.axis_size("tp")

    def body(q, qpos, kpos, *refs):
        block_refs, refs = refs[:n_blocks], refs[n_blocks:]
        w_ref, *outs, attended = refs
        x_lo = lax.axis_index("ctx") // n_half
        early = x_lo if layer == 0 else 1 - x_lo
        low = pl.ds(pl.multiple_of(early * half, half), half)
        high = pl.ds(pl.multiple_of((1 - early) * half, half), half)
        bias = jnp.where(kpos[...] <= qpos[...], 0.0, -1e30)
        ones = jnp.ones((keys, HS), jnp.bfloat16)

        def keys_of(rows_of, g):
            return jnp.concatenate(
                [b[rows_of, g * HS : (g + 1) * HS] for b in block_refs], axis=0
            )

        def values_of(rows_of, g):
            return jnp.concatenate([keys_of(rows_of, kv_heads + g), ones], axis=1)

        def score(qs, k):
            return lax.dot_general(
                qs, k, (((1,), (1,)), ((), ())), preferred_element_type=jnp.float32
            ).reshape(group, half, keys)

        def weigh(scores, best, v):
            weights = jnp.exp2(scores - best).astype(jnp.bfloat16)
            return jnp.dot(
                weights.reshape(group * half, keys), v, preferred_element_type=jnp.float32
            )

        for g in range(kv_heads):
            heads = [g * group + j for j in range(group)]
            k_low, k_high = keys_of(low, g), keys_of(high, g)
            v_low, v_high = values_of(low, g), values_of(high, g)
            q_low, q_high = (
                jnp.concatenate([q[r, h * HS : (h + 1) * HS] for h in heads], axis=0)
                for r in (low, high)
            )
            same = score(q_low, k_low) + bias[None]
            best = jnp.max(same, axis=-1, keepdims=True)
            acc_low = weigh(same, best, v_low)
            before = score(q_high, k_low)
            same = score(q_high, k_high) + bias[None]
            best = jnp.maximum(
                jnp.max(before, axis=-1, keepdims=True), jnp.max(same, axis=-1, keepdims=True)
            )
            acc_high = weigh(before, best, v_low) + weigh(same, best, v_high)
            for r, acc in ((low, acc_low), (high, acc_high)):
                normal = (acc[:, :HS] / acc[:, HS:]).astype(jnp.bfloat16)
                for j, h in enumerate(heads):
                    attended[r, h * HS : (h + 1) * HS] = normal[j * half : (j + 1) * half]
        project_parts(attended, w_ref, slice_width, width, parts, outs)

    got = in_vmem(
        body,
        [q, qpos, kpos, *blocks, w_out],
        [((n, width), jnp.bfloat16) for *_, n in parts] + [((rows, q_cols), jnp.bfloat16)],
        "attend_and_project",
        flops=6 * rows * q_cols * keys + 2 * rows * w_out.size,
        beside=BESIDE_MIX,
    )
    return got[:-1], got[-1]


def project_parts(attended, w_ref, slice_width, width, parts, outs):
    done = {}
    for (at, shift, row, n), out in zip(parts, outs):
        if (at, shift) not in done:
            there = pl.ds(from_slice(-shift, at, slice_width), width)
            done[at, shift] = jnp.dot(
                attended[...], w_ref[0, :, there], preferred_element_type=jnp.float32
            ).astype(jnp.bfloat16)
        out[...] = done[at, shift][row : row + n]


def project_out(attended, w_out, width, parts):
    slice_width = w_out.shape[2] // lax.axis_size("tp")

    def body(a, w, *outs):
        project_parts(a, w, slice_width, width, parts, outs)

    return in_vmem(
        body,
        [attended, w_out],
        [((n, width), jnp.bfloat16) for *_, n in parts],
        "project_out",
        flops=2 * sum(n for *_, n in parts) * attended.shape[1] * width,
    )


def total_of(parts):
    total = parts[0][...].astype(jnp.float32)
    for p in parts[1:]:
        total = total + p[...].astype(jnp.float32)
    return total


def add_parts(x, at, parts):
    rows, width = parts[0].shape

    def body(*refs):
        *refs, x_ref, out = refs
        x = x_ref[:, at : at + width].astype(jnp.float32)
        out[...] = (x + total_of(refs)).astype(jnp.bfloat16)

    return in_vmem(body, [*parts, x], [((rows, width), jnp.bfloat16)], "add_parts")[0]


def last_cross(kept, x, parts):
    def body(*refs):
        *refs, kept_ref, x_ref, out = refs
        section = lax.axis_index("section")
        total = x_ref[...].astype(jnp.float32) + total_of(refs)
        out[...] = jnp.where(section == 0, kept_ref[...], total.astype(jnp.bfloat16))

    return in_vmem(body, [*parts, kept, x], [(x.shape, jnp.bfloat16)], "last_cross")[0]


def finish(kept, x, parts, cross):
    half, width = x.shape
    n_half = lax.axis_size("ctx") // 2

    def body(*refs):
        *refs, cross_ref, kept_ref, x_ref, out = refs
        section = lax.axis_index("section")
        x_lo = lax.axis_index("ctx") // n_half
        total = x_ref[...].astype(jnp.float32) + total_of(refs)
        own = jnp.where(section == 0, kept_ref[...], total.astype(jnp.bfloat16))
        own_first = x_lo == section
        out[0, 0] = jnp.where(own_first, own, cross_ref[...])
        out[0, 1] = jnp.where(own_first, cross_ref[...], own)

    return in_vmem(
        body, [*parts, cross, kept, x], [((1, 2, half, width), jnp.bfloat16)], "finish"
    )[0]


def per_device(tokens, norm_gain, wq, wk, wv, w_out):
    n_ctx = lax.axis_size("ctx")
    n_tp = lax.axis_size("tp")
    n_z = n_ctx // 4
    ctx = lax.axis_index("ctx")
    x_lo = ctx // (n_ctx // 2)
    z = (ctx // 2) % n_z
    core = ctx % 2
    half = tokens.shape[1]
    width = tokens.shape[2]
    starts = [sum(CHUNKS[:c]) for c in range(len(CHUNKS))]

    local = lax.iota(jnp.int32, half)

    def positions(z_of, core_of):
        base = (z_of * 2 + core_of) * half + local
        mine = x_lo * (n_ctx // 2) * half + base
        theirs = (1 - x_lo) * (n_ctx // 2) * half + base
        return jnp.concatenate([mine, theirs])

    z_of = [(z - s) % n_z for s in (0, *Z_ORDER)]
    positions_of = positions(z, core)
    qpos = ((z * 2 + core) * half + local)[:, None]
    kpos = jnp.concatenate(
        [(zs * 2 + c) * half + local for c in (core, 1 - core) for zs in z_of]
    )[None, :]

    def tables(qpos):
        pairs = lax.iota(jnp.int32, HS // 2).astype(jnp.float32)
        freqs = jnp.power(jnp.float32(500000.0), -2.0 * pairs / HS)
        angle = qpos.astype(jnp.float32)[:, None] * freqs[None, :]
        cosine = jnp.cos(angle)
        sine = jnp.sin(angle)
        return (
            jnp.concatenate([cosine, cosine], axis=1),
            jnp.concatenate([-sine, sine], axis=1),
        )

    def swapped(rows):
        return jnp.concatenate([rows[half : 2 * half], rows[:half]], axis=0)


    def mix(kv, make_q, w_out, width, layer, parts):
        theirs = send(kv, other_core=True)
        sent = {s: send(kv, by_z=s) for s in Z_ORDER}
        first = Z_ORDER[0]
        q, theirs, sent[first] = lax.optimization_barrier((make_q(), theirs, sent[first]))
        mine = [sent[s] for s in Z_ORDER]
        theirs = [theirs] + [send(block, other_core=True) for block in mine]
        blocks = [kv, *mine, *theirs]
        return attend_and_project(q, qpos, kpos, blocks, w_out, width, layer, parts)

    own, other = rows_of_segments(tokens)
    own_from = {s: send(own, by_tp=s) for s in (3, 1, 2)}
    other = send(other, other_half=True)
    positions_of, gain, qpos, kpos, other = lax.optimization_barrier(
        (positions_of, norm_gain, qpos, kpos, other)
    )
    gain = widened(gain)
    rope = tables(positions_of)
    other_from = {s: send(other, by_tp=s) for s in (3, 1, 2)}
    own_from[0], other_from[0] = own, other
    pieces = [(s, 0, [own_from[s], other_from[s]]) for s in (0, 1, 3, 2)]
    kv, r = project_kv(pieces, width, gain, wk, wv, None, rope)
    chunked = [[(at, s, 0, 2 * half) for s in SHIFTS] for at in starts]
    got, attended = mix(
        kv,
        lambda: project_q(pieces, width, gain, wq, r, rope),
        w_out,
        CHUNKS[0],
        0,
        chunked[0],
    )
    for c in range(1, len(CHUNKS)):
        got += project_out(attended, w_out, CHUNKS[c], chunked[c])
    x0 = stacked(own, other)
    sums = []
    for c in range(len(CHUNKS)):
        parts = []
        for s, block in zip(SHIFTS, got[c * n_tp : (c + 1) * n_tp]):
            parts.append(send(block, by_tp=s) if s else block)
        sums.append(add_parts(x0, starts[c], parts))

    rope = tuple(swapped(t) for t in rope)
    carry = None
    every = []
    came = []
    for c in range(len(CHUNKS)):
        last = c == len(CHUNKS) - 1
        came.append(send(sums[c], next_layer=True))
        x_from = {0: came[c]}
        if c in DIAG:
            x_from[2] = send(sums[c], next_layer=True, by_tp=2)
        for s in (1, 3) if c in DIAG else (3, 1, 2):
            x_from[s] = send(came[c], by_tp=s)
        pieces = [(s, starts[c], [x_from[s]]) for s in ORDER]
        every += pieces
        carry = project_kv(pieces, width, gain, wk, wv, carry, rope if last else None)
    kv, r = carry
    kept = jnp.concatenate(sums, axis=1)
    x1 = jnp.concatenate(came, axis=1)
    got, attended = mix(
        kv,
        lambda: project_q(every, width, gain, wq, r, rope),
        w_out,
        width,
        1,
        [(0, s, row, half) for row in (0, half) for s in SHIFTS],
    )
    rest = got[n_tp:]
    parts = [send(block, by_tp=s) if s else block for s, block in zip(SHIFTS, got)]
    cross = send(last_cross(kept[half:], x1[:half], parts), other_half=True)
    parts = [send(block, by_tp=s) if s else block for s, block in zip(SHIFTS, rest)]
    return finish(kept[:half], x1[half:], parts, cross)


def solution(mesh):
    return jax.shard_map(
        per_device,
        mesh=mesh,
        in_specs=(
            P(None, "ctx", "tp"),
            P("section", None),
            P("section", None, "tp"),
            P("section", None, "tp"),
            P("section", None, "tp"),
            P("section", "tp", None),
        ),
        out_specs=P("section", None, "ctx", "tp"),
        check_vma=False,
    )
```

```python
import itertools
import math
import jax
import jax.numpy as jnp
from jax import lax
from jax.experimental import pallas as pl
from jax.experimental.pallas import tpu as pltpu
from jax.sharding import PartitionSpec as P

HS = 128
EPS = 1e-05
CHUNKS = (512, 512)
SMALL = 10 * 1024 * 1024
SHIFTS = (2, 1, 3, 0)
ORDER = (2, 0, 3, 1)
Z_ORDER = (3, 1, 2)
FLOPS_PER_US = 1_150_000_000
BESIDE_GAIN = 3
BESIDE_FIRST, BESIDE_KV, BESIDE_Q, BESIDE_MIX = 5, 2, 4, 8
DIAG = (0, 1)
AXES = ("section", "ctx", "tp")


def send(block, by_tp=0, by_z=0, other_half=False, other_core=False, next_layer=False):
    n_section = lax.axis_size("section")
    n_ctx = lax.axis_size("ctx")
    n_tp = lax.axis_size("tp")
    n_half = n_ctx // 2
    route = []
    for e, c, t in itertools.product(range(n_section), range(n_ctx), range(n_tp)):
        there = (c % n_half + 2 * by_z) % n_half + c // n_half * n_half
        if other_half or next_layer:
            there = (there + n_half) % n_ctx
        if other_core:
            there = there ^ 1
        end = (e + next_layer) % n_section
        route.append(
            ((e * n_ctx + c) * n_tp + t, (end * n_ctx + there) * n_tp + (t + by_tp) % n_tp)
        )
    return lax.ppermute(block, AXES, route)


def in_vmem(kernel, operands, out_shape, name, in_hbm=(), scratch=(), flops=0, beside=0):
    n_bytes = sum(x.size * x.dtype.itemsize for x in (*operands, *in_hbm))
    specs = [pl.BlockSpec(memory_space=pltpu.VMEM)] * len(operands)
    specs += [pl.BlockSpec(memory_space=pl.ANY)] * len(in_hbm)
    return pl.pallas_call(
        kernel,
        in_specs=specs,
        out_specs=[pl.BlockSpec(memory_space=pltpu.VMEM)] * len(out_shape),
        out_shape=[jax.ShapeDtypeStruct(shape, dtype) for shape, dtype in out_shape],
        scratch_shapes=list(scratch),
        compiler_params=pltpu.CompilerParams(vmem_limit_bytes=SMALL),
        cost_estimate=pl.CostEstimate(flops=flops + beside * FLOPS_PER_US, bytes_accessed=n_bytes, transcendentals=0),
        name=name,
    )(*operands, *[pltpu.with_memory_space_constraint(w, pltpu.HBM) for w in in_hbm])


def from_slice(shift, at, width):
    n_tp = lax.axis_size("tp")
    tp = lax.axis_index("tp")
    return pl.multiple_of(lax.rem(tp + (n_tp - shift) % n_tp, n_tp) * width + at, HS)


def scaled_piece(rows_of, gain, start):
    x = jnp.concatenate([r[...] for r in rows_of], axis=0).astype(jnp.float32)
    g = gain[:, pl.ds(start, x.shape[1])]
    return (x * g).astype(jnp.bfloat16), jnp.sum(x * x, axis=-1, keepdims=True)


def rotated(u, cos, sin):
    return u * cos + pltpu.roll(u, HS // 2, 1) * sin


def flat_pieces(pieces):
    most = max(len(rows_of) for _, _, rows_of in pieces)
    return [rows_of[n] for n in range(most) for _, _, rows_of in pieces if n < len(rows_of)]


def regroup(refs, pieces):
    out = [[] for _ in pieces]
    at = 0
    for n in range(max(len(rows_of) for _, _, rows_of in pieces)):
        for j, (_, _, rows_of) in enumerate(pieces):
            if n < len(rows_of):
                out[j].append(refs[at])
                at += 1
    return out, refs[at:]


def rows_of_segments(tokens):
    _, half, width = tokens.shape
    n_half = lax.axis_size("ctx") // 2

    def body(tokens_ref, own, other, sems):
        x_lo = lax.axis_index("ctx") // n_half
        copies = [
            pltpu.make_async_copy(tokens_ref.at[x_lo], own, sems.at[0]),
            pltpu.make_async_copy(tokens_ref.at[1 - x_lo], other, sems.at[1]),
        ]
        for c in copies:
            c.start()
        for c in copies:
            c.wait()

    return in_vmem(
        body,
        [],
        [((half, width), tokens.dtype)] * 2,
        "rows_of_segments",
        in_hbm=[tokens],
        scratch=[pltpu.SemaphoreType.DMA((2,))],
        beside=BESIDE_FIRST,
    )


def stacked(upper, lower):
    rows, width = upper.shape

    def body(a, b, out):
        out[:rows] = a[...]
        out[rows:] = b[...]

    return in_vmem(
        body, [upper, lower], [((2 * rows, width), upper.dtype)], "stacked"
    )[0]


def widened(gain):
    def body(g, out):
        out[...] = g[...].astype(jnp.float32)

    return in_vmem(
        body, [gain], [(gain.shape, jnp.float32)], "widened", beside=BESIDE_GAIN
    )[0]


def project_kv(pieces, slice_width, gain, wk, wv, carry, rope):
    rows = sum(x.shape[0] for x in pieces[0][2])
    width = pieces[0][2][0].shape[1]
    kv_cols = wk.shape[2]
    n = len(pieces)
    first, last = carry is None, rope is not None

    def body(*refs):
        groups, refs = regroup(refs, pieces)
        gain_ref, wk_ref, wv_ref = refs[:3]
        refs = refs[3:]
        ss = k = v = None
        if not first:
            acc_in, ss_in = refs[:2]
            refs = refs[2:]
            ss, k, v = ss_in[...], acc_in[:, :kv_cols], acc_in[:, kv_cols:]
        for (shift, at, _), rows_of in zip(pieces, groups):
            start = from_slice(shift, at, slice_width)
            x, squares = scaled_piece(rows_of, gain_ref, start)
            here = pl.ds(start, width)
            pk = jnp.dot(x, wk_ref[0, here, :], preferred_element_type=jnp.float32)
            pv = jnp.dot(x, wv_ref[0, here, :], preferred_element_type=jnp.float32)
            ss = squares if ss is None else ss + squares
            k = pk if k is None else k + pk
            v = pv if v is None else v + pv
        if last:
            cos, sin, out, r_out = refs
            r = lax.rsqrt(ss / 4096.0 + EPS)
            r_out[...] = r
            for h in range(kv_cols // HS):
                at = slice(h * HS, (h + 1) * HS)
                out[:, at] = rotated(k[:, at] * r, cos[...], sin[...]).astype(jnp.bfloat16)
            out[:, kv_cols:] = (v * r).astype(jnp.bfloat16)
        else:
            acc, ss_out = refs
            acc[:, :kv_cols] = k
            acc[:, kv_cols:] = v
            ss_out[...] = ss

    operands = flat_pieces(pieces) + [gain, wk, wv]
    operands += [] if first else list(carry)
    operands += list(rope) if last else []
    kind = jnp.bfloat16 if last else jnp.float32
    return in_vmem(
        body,
        operands,
        [((rows, 2 * kv_cols), kind), ((rows, 1), jnp.float32)],
        "project_kv",
        flops=4 * rows * n * width * kv_cols,
        beside=BESIDE_KV,
    )


def project_q(pieces, slice_width, gain, wq, r, rope):
    rows = sum(x.shape[0] for x in pieces[0][2])
    width = pieces[0][2][0].shape[1]
    cols = wq.shape[2]

    def body(*refs):
        groups, refs = regroup(refs, pieces)
        gain_ref, w_ref, r_ref, cos, sin, out = refs
        acc = None
        for (shift, at, _), rows_of in zip(pieces, groups):
            start = from_slice(shift, at, slice_width)
            x, _ = scaled_piece(rows_of, gain_ref, start)
            part = jnp.dot(
                x, w_ref[0, pl.ds(start, width), :], preferred_element_type=jnp.float32
            )
            acc = part if acc is None else acc + part
        r = r_ref[...] * (math.log2(math.e) / math.sqrt(HS))
        for h in range(cols // HS):
            at = slice(h * HS, (h + 1) * HS)
            out[:, at] = rotated(acc[:, at] * r, cos[...], sin[...]).astype(jnp.bfloat16)

    return in_vmem(
        body,
        flat_pieces(pieces) + [gain, wq, r, *rope],
        [((rows, cols), jnp.bfloat16)],
        "project_q",
        flops=2 * rows * wq.size,
        beside=BESIDE_Q,
    )[0]


def attend_and_project(q, qpos, kpos, blocks, w_out, width, layer, parts):
    rows, q_cols = q.shape
    kv_heads = blocks[0].shape[1] // (2 * HS)
    group = q_cols // HS // kv_heads
    n_blocks = len(blocks)
    half = rows // 2
    keys = half * n_blocks
    n_half = lax.axis_size("ctx") // 2
    slice_width = w_out.shape[2] // lax.axis_size("tp")

    def body(q, qpos, kpos, *refs):
        block_refs, refs = refs[:n_blocks], refs[n_blocks:]
        w_ref, *outs, attended = refs
        x_lo = lax.axis_index("ctx") // n_half
        early = x_lo if layer == 0 else 1 - x_lo
        low = pl.ds(pl.multiple_of(early * half, half), half)
        high = pl.ds(pl.multiple_of((1 - early) * half, half), half)
        bias = jnp.where(kpos[...] <= qpos[...], 0.0, -1e30)
        ones = jnp.ones((keys, HS), jnp.bfloat16)

        def keys_of(rows_of, g):
            return jnp.concatenate(
                [b[rows_of, g * HS : (g + 1) * HS] for b in block_refs], axis=0
            )

        def values_of(rows_of, g):
            return jnp.concatenate([keys_of(rows_of, kv_heads + g), ones], axis=1)

        def score(qs, k):
            return lax.dot_general(
                qs, k, (((1,), (1,)), ((), ())), preferred_element_type=jnp.float32
            ).reshape(group, half, keys)

        def weigh(scores, best, v):
            weights = jnp.exp2(scores - best).astype(jnp.bfloat16)
            return jnp.dot(
                weights.reshape(group * half, keys), v, preferred_element_type=jnp.float32
            )

        for g in range(kv_heads):
            heads = [g * group + j for j in range(group)]
            k_low, k_high = keys_of(low, g), keys_of(high, g)
            v_low, v_high = values_of(low, g), values_of(high, g)
            q_low, q_high = (
                jnp.concatenate([q[r, h * HS : (h + 1) * HS] for h in heads], axis=0)
                for r in (low, high)
            )
            same = score(q_low, k_low) + bias[None]
            best = jnp.max(same, axis=-1, keepdims=True)
            acc_low = weigh(same, best, v_low)
            before = score(q_high, k_low)
            same = score(q_high, k_high) + bias[None]
            best = jnp.maximum(
                jnp.max(before, axis=-1, keepdims=True), jnp.max(same, axis=-1, keepdims=True)
            )
            acc_high = weigh(before, best, v_low) + weigh(same, best, v_high)
            for r, acc in ((low, acc_low), (high, acc_high)):
                normal = (acc[:, :HS] / acc[:, HS:]).astype(jnp.bfloat16)
                for j, h in enumerate(heads):
                    attended[r, h * HS : (h + 1) * HS] = normal[j * half : (j + 1) * half]
        project_parts(attended, w_ref, slice_width, width, parts, outs)

    got = in_vmem(
        body,
        [q, qpos, kpos, *blocks, w_out],
        [((n, width), jnp.bfloat16) for *_, n in parts] + [((rows, q_cols), jnp.bfloat16)],
        "attend_and_project",
        flops=6 * rows * q_cols * keys + 2 * rows * w_out.size,
        beside=BESIDE_MIX,
    )
    return got[:-1], got[-1]


def project_parts(attended, w_ref, slice_width, width, parts, outs):
    done = {}
    for (at, shift, row, n), out in zip(parts, outs):
        if (at, shift) not in done:
            there = pl.ds(from_slice(-shift, at, slice_width), width)
            done[at, shift] = jnp.dot(
                attended[...], w_ref[0, :, there], preferred_element_type=jnp.float32
            ).astype(jnp.bfloat16)
        out[...] = done[at, shift][row : row + n]


def project_out(attended, w_out, width, parts):
    slice_width = w_out.shape[2] // lax.axis_size("tp")

    def body(a, w, *outs):
        project_parts(a, w, slice_width, width, parts, outs)

    return in_vmem(
        body,
        [attended, w_out],
        [((n, width), jnp.bfloat16) for *_, n in parts],
        "project_out",
        flops=2 * sum(n for *_, n in parts) * attended.shape[1] * width,
    )


def total_of(parts):
    total = parts[0][...].astype(jnp.float32)
    for p in parts[1:]:
        total = total + p[...].astype(jnp.float32)
    return total


def add_parts(x, at, parts):
    rows, width = parts[0].shape

    def body(*refs):
        *refs, x_ref, out = refs
        x = x_ref[:, at : at + width].astype(jnp.float32)
        out[...] = (x + total_of(refs)).astype(jnp.bfloat16)

    return in_vmem(body, [*parts, x], [((rows, width), jnp.bfloat16)], "add_parts")[0]


def last_cross(kept, x, parts):
    def body(*refs):
        *refs, kept_ref, x_ref, out = refs
        section = lax.axis_index("section")
        total = x_ref[...].astype(jnp.float32) + total_of(refs)
        out[...] = jnp.where(section == 0, kept_ref[...], total.astype(jnp.bfloat16))

    return in_vmem(body, [*parts, kept, x], [(x.shape, jnp.bfloat16)], "last_cross")[0]


def finish(kept, x, parts, cross):
    half, width = x.shape
    n_half = lax.axis_size("ctx") // 2

    def body(*refs):
        *refs, cross_ref, kept_ref, x_ref, out = refs
        section = lax.axis_index("section")
        x_lo = lax.axis_index("ctx") // n_half
        total = x_ref[...].astype(jnp.float32) + total_of(refs)
        own = jnp.where(section == 0, kept_ref[...], total.astype(jnp.bfloat16))
        own_first = x_lo == section
        out[0, 0] = jnp.where(own_first, own, cross_ref[...])
        out[0, 1] = jnp.where(own_first, cross_ref[...], own)

    return in_vmem(
        body, [*parts, cross, kept, x], [((1, 2, half, width), jnp.bfloat16)], "finish"
    )[0]


def per_device(tokens, norm_gain, wq, wk, wv, w_out):
    n_ctx = lax.axis_size("ctx")
    n_tp = lax.axis_size("tp")
    n_z = n_ctx // 4
    ctx = lax.axis_index("ctx")
    x_lo = ctx // (n_ctx // 2)
    z = (ctx // 2) % n_z
    core = ctx % 2
    half = tokens.shape[1]
    width = tokens.shape[2]
    starts = [sum(CHUNKS[:c]) for c in range(len(CHUNKS))]

    local = lax.iota(jnp.int32, half)

    def positions(z_of, core_of):
        base = (z_of * 2 + core_of) * half + local
        mine = x_lo * (n_ctx // 2) * half + base
        theirs = (1 - x_lo) * (n_ctx // 2) * half + base
        return jnp.concatenate([mine, theirs])

    z_of = [(z - s) % n_z for s in (0, *Z_ORDER)]
    positions_of = positions(z, core)
    qpos = ((z * 2 + core) * half + local)[:, None]
    kpos = jnp.concatenate(
        [(zs * 2 + c) * half + local for c in (core, 1 - core) for zs in z_of]
    )[None, :]

    def tables(qpos):
        pairs = lax.iota(jnp.int32, HS // 2).astype(jnp.float32)
        freqs = jnp.power(jnp.float32(500000.0), -2.0 * pairs / HS)
        angle = qpos.astype(jnp.float32)[:, None] * freqs[None, :]
        cosine = jnp.cos(angle)
        sine = jnp.sin(angle)
        return (
            jnp.concatenate([cosine, cosine], axis=1),
            jnp.concatenate([-sine, sine], axis=1),
        )

    def swapped(rows):
        return jnp.concatenate([rows[half : 2 * half], rows[:half]], axis=0)


    def mix(kv, make_q, w_out, width, layer, parts):
        theirs = send(kv, other_core=True)
        sent = {s: send(kv, by_z=s) for s in Z_ORDER}
        first = Z_ORDER[0]
        q, theirs, sent[first] = lax.optimization_barrier((make_q(), theirs, sent[first]))
        mine = [sent[s] for s in Z_ORDER]
        theirs = [theirs] + [send(block, other_core=True) for block in mine]
        blocks = [kv, *mine, *theirs]
        return attend_and_project(q, qpos, kpos, blocks, w_out, width, layer, parts)

    own, other = rows_of_segments(tokens)
    own_from = {s: send(own, by_tp=s) for s in (3, 1, 2)}
    other = send(other, other_half=True)
    positions_of, gain, qpos, kpos, other = lax.optimization_barrier(
        (positions_of, norm_gain, qpos, kpos, other)
    )
    gain = widened(gain)
    rope = tables(positions_of)
    other_from = {s: send(other, by_tp=s) for s in (3, 1, 2)}
    own_from[0], other_from[0] = own, other
    pieces = [(s, 0, [own_from[s], other_from[s]]) for s in (0, 1, 3, 2)]
    kv, r = project_kv(pieces, width, gain, wk, wv, None, rope)
    chunked = [[(at, s, 0, 2 * half) for s in SHIFTS] for at in starts]
    got, attended = mix(
        kv,
        lambda: project_q(pieces, width, gain, wq, r, rope),
        w_out,
        CHUNKS[0],
        0,
        chunked[0],
    )
    for c in range(1, len(CHUNKS)):
        got += project_out(attended, w_out, CHUNKS[c], chunked[c])
    x0 = stacked(own, other)
    sums = []
    for c in range(len(CHUNKS)):
        parts = []
        for s, block in zip(SHIFTS, got[c * n_tp : (c + 1) * n_tp]):
            parts.append(send(block, by_tp=s) if s else block)
        sums.append(add_parts(x0, starts[c], parts))

    rope = tuple(swapped(t) for t in rope)
    carry = None
    every = []
    came = []
    for c in range(len(CHUNKS)):
        last = c == len(CHUNKS) - 1
        came.append(send(sums[c], next_layer=True))
        x_from = {0: came[c]}
        if c in DIAG:
            x_from[2] = send(sums[c], next_layer=True, by_tp=2)
        for s in (1, 3) if c in DIAG else (3, 1, 2):
            x_from[s] = send(came[c], by_tp=s)
        pieces = [(s, starts[c], [x_from[s]]) for s in ORDER]
        every += pieces
        carry = project_kv(pieces, width, gain, wk, wv, carry, rope if last else None)
    kv, r = carry
    kept = jnp.concatenate(sums, axis=1)
    x1 = jnp.concatenate(came, axis=1)
    got, attended = mix(
        kv,
        lambda: project_q(every, width, gain, wq, r, rope),
        w_out,
        width,
        1,
        [(0, s, row, half) for row in (0, half) for s in SHIFTS],
    )
    rest = got[n_tp:]
    parts = [send(block, by_tp=s) if s else block for s, block in zip(SHIFTS, got)]
    cross = send(last_cross(kept[half:], x1[:half], parts), other_half=True)
    parts = [send(block, by_tp=s) if s else block for s, block in zip(SHIFTS, rest)]
    return finish(kept[:half], x1[half:], parts, cross)


def solution(mesh):
    return jax.shard_map(
        per_device,
        mesh=mesh,
        in_specs=(
            P(None, "ctx", "tp"),
            P("section", None),
            P("section", None, "tp"),
            P("section", None, "tp"),
            P("section", None, "tp"),
            P("section", "tp", None),
        ),
        out_specs=P("section", None, "ctx", "tp"),
        check_vma=False,
    )
```
